512 devices in a mesh: client: 32 (over x_hi, z, core), fsdp: 16 (over y, x_lo).
Axes of the slice: x: 4 (x_hi: 2, x_lo: 2; x = x_hi * 2 + x_lo), y: 8, z: 8, core: 2. Of those that a mesh axis runs over, the one named last changes fastest.
Arguments:
- head_outputs: bfloat16 [65536, 2048], P(('client', 'fsdp')), may hold values from -13 to 13
- out_weight: bfloat16 [2048, 4608], P(None, 'fsdp'), as said below
- norm_gain: float32 [4608], P('fsdp'), may hold values from 0.5 to 1.5
- cotangent: bfloat16 [65536, 4608], P(('client', 'fsdp')), may hold values from -17 to 17
- loss_mask: int32 [65536], P(('client', 'fsdp')), may hold values 0 or 1
- weight_noise: float32 [2048, 4608], P('client', 'fsdp'), may hold values from -12 to 12
- gain_noise: float32 [4608], P('fsdp'), may hold values from -12 to 12
Outputs:
- weight_update: float32 [2048, 4608], P('client', 'fsdp')
- gain_update: float32 [4608], P('fsdp')
The draws below stay inside these ranges and needn't reach their ends.
Inputs may be any that keep to these rules, and one draw needn't show every extreme that they name: `out_weight`: real-valued projection entries, each within 8.4 / sqrt(2048) of zero.
All inputs are finite; a program needn't handle non-finite values. No bound on the sum of `loss_mask` on one device may be relied on, other than what follows from the above.
Results may differ from the reference program's by a relative error of at most 0.0027.
Values may be sent and summed in bfloat16 or wider, within the bound.
No kernel may reach another device: no remote copies, remote signals or barrier semaphores. Data moves between devices by JAX's collectives and lax.ppermute only.
A program may use at most 64 MiB of HBM per device.

```python
import math
import jax
import jax.numpy as jnp
from jax import lax

D = 4608
HD = 2048
TOKENS = 65536
N_CLIENT = 32


def column_ramp(amount):
    steps = jnp.arange(amount, dtype=jnp.float32) / max(amount - 1, 1)
    return 1.0 + steps


def log_spread(key, amount, lower, upper):
    return jnp.exp(jax.random.uniform(key, (amount,), jnp.float32, math.log(lower), math.log(upper)))


def draw_head_outputs(key, part):
    key = jax.random.fold_in(key, 11)
    first, second = jax.random.split(key, 2)
    scales = log_spread(second, HD, 0.32, 3.2)
    base = jax.random.truncated_normal(first, -4.0, 4.0, (TOKENS, HD), jnp.float32)
    return (base * scales).astype(jnp.bfloat16)


def draw_cotangent(key, part):
    key = jax.random.fold_in(key, 23)
    first, second = jax.random.split(key, 2)
    scales = column_ramp(D) * log_spread(second, D, 0.5, 2.0)
    base = jax.random.truncated_normal(first, -4.0, 4.0, (TOKENS, D), jnp.float32)
    return (base * scales).astype(jnp.bfloat16)


def draw_out_weight(key, part):
    key = jax.random.fold_in(key, 37)
    first, second = jax.random.split(key, 2)
    scales = column_ramp(D) * jax.random.uniform(second, (D,), jnp.float32, 0.6, 1.4)
    base = jax.random.truncated_normal(first, -3.0, 3.0, (HD, D), jnp.float32)
    return (base * scales / math.sqrt(HD)).astype(jnp.bfloat16)


def touch_ends(array, own_key, least, high):
    place = [jax.random.randint(jax.random.fold_in(own_key, axis), (), 0, length) for axis, length in enumerate(array.shape)]
    main_axis = array.shape.index(max(array.shape))
    neighbour = place[:main_axis] + [(place[main_axis] + 1) % array.shape[main_axis]] + place[main_axis + 1:]
    return array.at[tuple(place)].set(least).at[tuple(neighbour)].set(high)


def shard_levels(own_key, shape, cuts, smallest, largest):
    def one(position, blocks):
        heights = jax.random.uniform(jax.random.fold_in(jax.random.fold_in(own_key, 6), position), (blocks,), jnp.float32, smallest / len(cuts), largest / len(cuts))
        return jnp.repeat(jnp.exp(heights), shape[position] // blocks).reshape((-1,) + (1,) * (len(shape) - position - 1))

    level = one(*cuts[0])
    for cut in cuts[1:]:
        level = level * one(*cut)
    return level


def centred(rng, shape, deviation, bound, cuts=(), kind=jnp.bfloat16):
    factor_of = shard_levels(rng, shape, cuts, -0.22, 0.18) if cuts else 1.0
    result = jax.random.normal(rng, shape, jnp.float32) * deviation * factor_of
    return jnp.minimum(jnp.maximum(result, -bound), bound).astype(kind)


def setup_inputs(seed: int = 0) -> dict:
    seeds = jax.random.split(jax.random.key(seed), 8)
    head_outputs = draw_head_outputs(jax.random.fold_in(seeds[7], 71), 0)
    out_weight = draw_out_weight(jax.random.fold_in(seeds[7], 71), 0)
    norm_gain = jnp.clip(0.5 + 1.0 * jax.random.uniform(seeds[2], (D,), jnp.float32) ** shard_levels(seeds[2], (D,), ((0, 16),), -0.2, 0.2), 0.5, 1.5)
    cotangent = draw_cotangent(jax.random.fold_in(seeds[7], 71), 0)
    loss_mask = touch_ends((jax.random.randint(seeds[4], (TOKENS,), 0, 4) < 3).astype(jnp.int32), jax.random.fold_in(seeds[4], 1), 0, 1)
    weight_noise = centred(seeds[5], (HD, D), 2.0, 12.0, ((0, 32), (1, 16)), jnp.float32)
    gain_noise = centred(seeds[6], (D,), 2.0, 12.0, ((0, 16),), jnp.float32)
    return {"head_outputs": head_outputs, "out_weight": out_weight, "norm_gain": norm_gain, "cotangent": cotangent, "loss_mask": loss_mask, "weight_noise": weight_noise, "gain_noise": gain_noise}


epsilon = 1e-06

def client_delta(heads_block, cot_block, mask_block, out_weight, norm_gain):
    projected = jnp.dot(heads_block, out_weight, preferred_element_type=jnp.float32)
    inverse = lax.rsqrt(lax.optimization_barrier(jnp.mean(projected * projected, axis=1, keepdims=True)) + epsilon)
    masked = (cot_block * mask_block[:, None].astype(jnp.bfloat16)).astype(jnp.float32)
    products = lax.optimization_barrier(jnp.sum(projected * norm_gain * masked, axis=1, keepdims=True))
    back_grad = (inverse * norm_gain * masked - projected * inverse * inverse * inverse * products / D).astype(jnp.bfloat16)
    weight_grad = jnp.dot(heads_block.T, back_grad, preferred_element_type=jnp.float32)
    gain_grad = lax.optimization_barrier(jnp.sum(masked * projected * inverse, axis=0))
    norm_sq = jnp.sum(weight_grad * weight_grad) + jnp.sum(gain_grad * gain_grad)
    clip_bound = math.sqrt(HD * D)
    factor = clip_bound / jnp.maximum(jnp.sqrt(norm_sq), clip_bound)
    return (weight_grad * factor, gain_grad * factor)

def reference(head_outputs, out_weight, norm_gain, cotangent, loss_mask, weight_noise, gain_noise):
    clients = N_CLIENT
    client_tokens = head_outputs.shape[0] // clients
    heads_split = head_outputs.reshape(clients, client_tokens, HD)
    cot_split = cotangent.reshape(clients, client_tokens, D)
    mask_split = loss_mask.reshape(clients, client_tokens)

    def accumulate(carry, pieces):
        weight_term, gain_term = client_delta(pieces[0], pieces[1], pieces[2], out_weight, norm_gain)
        return ((carry[0] + weight_term, carry[1] + gain_term), None)
    initial = (jnp.zeros((HD, D), jnp.float32), jnp.zeros((D,), jnp.float32))
    totals, _ = lax.scan(accumulate, initial, (heads_split, cot_split, mask_split))
    weight_update = (totals[0] + weight_noise) / clients
    gain_update = (totals[1] + gain_noise) / clients
    return (weight_update, gain_update)
```

```python
import math

import jax
import jax.numpy as jnp
from jax import lax
from jax.sharding import Mesh, PartitionSpec as P

D = 4608
HD = 2048
epsilon = 1e-06
CLIENT = ("xh", "z", "core")
FSDP = ("y", "xl")


def swap(x, axis):
    return lax.ppermute(x, axis, [(0, 1), (1, 0)])


def local(head_outputs, out_weight, norm_gain, cotangent, loss_mask, weight_noise, gain_noise):
    xl = lax.axis_index("xl")
    core = lax.axis_index("core")
    xh = lax.axis_index("xh")
    clients = 32.0
    heads = lax.all_gather(head_outputs, "y", axis=0, tiled=True)
    masked = cotangent * loss_mask[:, None].astype(jnp.bfloat16)
    pieces = masked.reshape(128, 8, 2, 288).transpose(1, 2, 3, 0)
    low, high = pieces[:, 0], pieces[:, 1]
    ordered = jnp.concatenate(
        [jnp.where(xl == 0, low, high), jnp.where(xl == 0, high, low)], axis=1
    )
    arrived = lax.all_to_all(ordered, "y", split_axis=0, concat_axis=0, tiled=True)
    arrived = arrived.transpose(1, 0, 2).reshape(576, 1024).astype(jnp.float32)
    weight_t = out_weight.T
    weights = jnp.concatenate([weight_t, swap(weight_t, "xl")], axis=0)
    gain = jnp.concatenate([norm_gain, swap(norm_gain, "xl")])[:, None]
    projected = lax.dot_general(
        weights, heads, (((1,), (1,)), ((), ())), preferred_element_type=jnp.float32
    )
    stats = jnp.stack(
        [jnp.sum(projected * projected, axis=0), jnp.sum(projected * gain * arrived, axis=0)]
    )
    stats = jnp.sum(
        lax.all_to_all(
            jnp.broadcast_to(stats[None], (8, 2, 1024)), "y", split_axis=0, concat_axis=0, tiled=True
        ),
        axis=0,
    )
    inverse = lax.rsqrt(stats[0:1] / D + epsilon)
    products = stats[1:2]
    back_grad = (
        inverse * gain * arrived - projected * (inverse * inverse * inverse * products / D)
    ).astype(jnp.bfloat16)
    gain_part = jnp.sum(arrived * projected * inverse, axis=1)
    partial = lax.dot_general(
        back_grad, heads, (((1,), (0,)), ((), ())), preferred_element_type=jnp.float32
    )
    sent = swap(partial[288:].astype(jnp.bfloat16), "xl")
    weight_grad = partial[:288] + sent.astype(jnp.float32)
    gain_grad = gain_part[:288] + swap(gain_part[288:], "xl")
    local_sum = jnp.sum(weight_grad * weight_grad) + jnp.sum(gain_grad * gain_grad)
    sums = lax.all_to_all(
        jnp.broadcast_to(local_sum, (32, 128)), ("core", "y", "xl"), split_axis=0, concat_axis=0, tiled=True
    )
    norms = jnp.sum(sums.reshape(2, 16, 128)[:, :, 0], axis=1)
    clip_bound = math.sqrt(HD * D)
    factors = clip_bound / jnp.maximum(jnp.sqrt(norms), clip_bound)
    mine = jnp.where(core == 0, factors[0], factors[1])
    other = jnp.where(core == 0, factors[1], factors[0])
    rows = weight_grad.reshape(288, 2, 8, 2, 64).transpose(3, 2, 0, 1, 4).reshape(2, 8, 288, 128)
    keep = jnp.where(core == 0, rows[0], rows[1])
    give = jnp.where(core == 0, rows[1], rows[0])
    gain_pair = mine * gain_grad + other * swap(gain_grad, "core")
    chip = (mine * keep + other * swap(give, "core")).astype(jnp.bfloat16)
    gain_high = gain_pair.astype(jnp.bfloat16)
    gain_low = (gain_pair - gain_high.astype(jnp.float32)).astype(jnp.bfloat16)
    extra = jnp.pad(jnp.stack([gain_high, gain_low]), ((0, 0), (0, 96))).reshape(6, 128)
    extra = jnp.broadcast_to(jnp.pad(extra, ((0, 10), (0, 0)))[None], (8, 16, 128))
    over_z = lax.all_to_all(
        jnp.concatenate([chip, extra], axis=1), "z", split_axis=0, concat_axis=0, tiled=True
    )
    column = jnp.sum(over_z.astype(jnp.float32), axis=0)
    gain_column = (column[288:291] + column[291:294])
    column = jnp.concatenate([column[:288], gain_column], axis=0)
    column2 = column + swap(column, "xh")
    mine_rows = jnp.where(xh == 0, column2[:288, :64], column2[:288, 64:])
    gain_sum = column2[288:].reshape(384)[:288]
    return ((mine_rows.T + weight_noise) / clients, (gain_sum + gain_noise) / clients)


def solution(mesh):
    split = Mesh(mesh.devices.reshape(2, 8, 2, 8, 2), CLIENT + FSDP)
    both = CLIENT + FSDP
    placed = (
        P(both, None),
        P(None, FSDP),
        P(FSDP),
        P(both, None),
        P(both),
        P(CLIENT, FSDP),
        P(FSDP),
    )
    return jax.shard_map(
        local,
        mesh=split,
        in_specs=placed,
        out_specs=(P(CLIENT, FSDP), P(FSDP)),
        check_vma=False,
    )
```

```python
import functools
import math

import jax
import jax.numpy as jnp
from jax import lax
from jax.experimental import pallas as pl
from jax.experimental.pallas import tpu as pltpu
from jax.sharding import Mesh, PartitionSpec as P

D = 4608
HD = 2048
epsilon = 1e-06
CLIENT = ("xh", "z", "core")
FSDP = ("y", "xl")
BOUND = math.sqrt(HD * D)
f32 = jnp.float32
bf16 = jnp.bfloat16


def swap(x, axis):
    return lax.ppermute(x, axis, [(0, 1), (1, 0)])


def full(shape):
    return pl.BlockSpec(shape, lambda *i: (0,) * len(shape))


def split_kernel(core_ref, own_ref, other_ref, gown_ref, gother_ref, keep_ref, give_ref, gain_ref, sum_ref, total):
    step = pl.program_id(0)
    block = own_ref[...] + other_ref[...].astype(f32)
    squares = block * block

    @pl.when(step == 0)
    def _():
        total[...] = squares

    @pl.when(step > 0)
    def _():
        total[...] += squares

    low, high = block[:144], block[144:]
    left = lax.broadcasted_iota(jnp.int32, (144, 128), 1) < 64
    first = jnp.where(left, low, pltpu.roll(high, 64, 1))
    second = jnp.where(left, pltpu.roll(low, 64, 1), high)
    zero = core_ref[0] == 0
    keep_ref[0] = jnp.where(zero, first, second)
    give_ref[0] = jnp.where(zero, second, first)

    @pl.when(step == pl.num_programs(0) - 1)
    def _():
        gain = gown_ref[...] + gother_ref[...]
        gain_ref[...] = gain
        sum_ref[...] = jnp.full((32, 128), jnp.sum(total[...]) + jnp.sum(gain * gain), f32)


def split(core, own, other, gown, gother):
    block = pl.BlockSpec((288, 128), lambda n: (0, n))
    half = pl.BlockSpec((1, 144, 128), lambda n: (n, 0, 0))
    return pl.pallas_call(
        split_kernel,
        grid=(16,),
        in_specs=[pl.BlockSpec(memory_space=pltpu.SMEM), block, block, full((3, 128)), full((3, 128))],
        out_specs=[half, half, full((3, 128)), full((32, 128))],
        out_shape=[
            jax.ShapeDtypeStruct((16, 144, 128), f32),
            jax.ShapeDtypeStruct((16, 144, 128), f32),
            jax.ShapeDtypeStruct((3, 128), f32),
            jax.ShapeDtypeStruct((32, 128), f32),
        ],
        scratch_shapes=[pltpu.VMEM((288, 128), f32)],
        name="split_by_core",
    )(core, own, other, gown, gother)


def combine_kernel(core_ref, sums_ref, keep_ref, got_ref, gown_ref, gother_ref, out_ref):
    norms = [jnp.sum(sums_ref[16 * i : 16 * i + 16], axis=0, keepdims=True) for i in range(2)]
    factors = [BOUND / jnp.maximum(jnp.sqrt(n), BOUND) for n in norms]
    zero = core_ref[0] == 0
    mine = jnp.where(zero, factors[0], factors[1])
    other = jnp.where(zero, factors[1], factors[0])
    gain = mine * gown_ref[...] + other * gother_ref[...]
    high = gain.astype(bf16).astype(f32)
    extra = jnp.concatenate([high, gain - high, jnp.zeros((10, 128), f32)], axis=0).astype(bf16)
    for i in range(out_ref.shape[0]):
        out_ref[i, :144] = (mine * keep_ref[i] + other * got_ref[i]).astype(bf16)
        out_ref[i, 144:] = extra


def combine(core, sums, keep, got, gown, gother):
    half = pl.BlockSpec((4, 144, 128), lambda n: (n, 0, 0))
    return pl.pallas_call(
        combine_kernel,
        grid=(4,),
        in_specs=[
            pl.BlockSpec(memory_space=pltpu.SMEM),
            full((32, 128)),
            half,
            half,
            full((3, 128)),
            full((3, 128)),
        ],
        out_specs=pl.BlockSpec((4, 160, 128), lambda n: (n, 0, 0)),
        out_shape=jax.ShapeDtypeStruct((16, 160, 128), bf16),
        name="clip_and_combine",
    )(core, sums, keep, got, gown, gother)


def finish_kernel(parts_ref, noise_ref, gain_noise_ref, out_ref, gain_ref):
    total = parts_ref[0].astype(f32)
    for i in range(1, 16):
        total = total + parts_ref[i].astype(f32)
    body = total[:144]
    rows = jnp.concatenate([body, pltpu.roll(body, 64, 1)], axis=0).T
    out_ref[...] = (rows[:64] + noise_ref[...]) * (1.0 / 32.0)
    gain_ref[...] = (total[144:147] + total[147:150] + gain_noise_ref[...]) * (1.0 / 32.0)


def finish(parts, noise, gain_noise):
    return pl.pallas_call(
        finish_kernel,
        out_shape=[jax.ShapeDtypeStruct((64, 288), f32), jax.ShapeDtypeStruct((3, 128), f32)],
        name="sum_and_noise",
    )(parts, noise, gain_noise)


def lanes(vector):
    return jnp.pad(vector, (0, 96)).reshape(3, 128)


def local(head_outputs, out_weight, norm_gain, cotangent, loss_mask, weight_noise, gain_noise):
    xl = lax.axis_index("xl")
    core = lax.axis_index("core").astype(jnp.int32).reshape(1)
    heads = lax.all_gather(head_outputs, "y", axis=0, tiled=True)
    masked = cotangent * loss_mask[:, None].astype(bf16)
    pieces = masked.reshape(128, 8, 2, 288).transpose(1, 2, 3, 0)
    low, high = pieces[:, 0], pieces[:, 1]
    ordered = jnp.concatenate(
        [jnp.where(xl == 0, low, high), jnp.where(xl == 0, high, low)], axis=1
    )
    arrived = lax.all_to_all(ordered, "y", split_axis=0, concat_axis=0, tiled=True)
    arrived = arrived.transpose(1, 0, 2).reshape(576, 1024).astype(f32)
    weight_t = out_weight.T
    weights = jnp.concatenate([weight_t, swap(weight_t, "xl")], axis=0)
    gain = jnp.concatenate([norm_gain, swap(norm_gain, "xl")])[:, None]
    projected = lax.dot_general(
        weights, heads, (((1,), (1,)), ((), ())), preferred_element_type=f32
    )
    stats = jnp.stack(
        [jnp.sum(projected * projected, axis=0), jnp.sum(projected * gain * arrived, axis=0)]
    )
    stats = jnp.sum(
        lax.all_to_all(
            jnp.broadcast_to(stats[None], (8, 2, 1024)), "y", split_axis=0, concat_axis=0, tiled=True
        ),
        axis=0,
    )
    inverse = lax.rsqrt(stats[0:1] / D + epsilon)
    products = stats[1:2]
    back_grad = (
        inverse * gain * arrived - projected * (inverse * inverse * inverse * products / D)
    ).astype(bf16)
    contract = (((1,), (0,)), ((), ()))
    other_part = lax.dot_general(back_grad[288:], heads, contract, preferred_element_type=f32)
    got_part = swap(other_part.astype(bf16), "xl")
    own_part = lax.dot_general(back_grad[:288], heads, contract, preferred_element_type=f32)
    gain_part = jnp.sum(arrived * projected * inverse, axis=1)
    gain_got = swap(lanes(gain_part[288:]), "xl")
    keep, give, gain_grad, squares = split(core, own_part, got_part, lanes(gain_part[:288]), gain_got)
    sums = lax.all_to_all(squares, ("core", "y", "xl"), split_axis=0, concat_axis=0, tiled=True)
    got = swap(give, "core")
    gain_other = swap(gain_grad, "core")
    chip = combine(core, sums, keep, got, gain_grad, gain_other)
    parts = lax.all_to_all(chip, ("xh", "z"), split_axis=0, concat_axis=0, tiled=True)
    update, gain_update = finish(parts, weight_noise, lanes(gain_noise))
    return update, gain_update.reshape(384)[:288]


def solution(mesh):
    split_mesh = Mesh(mesh.devices.reshape(2, 8, 2, 8, 2), CLIENT + FSDP)
    both = CLIENT + FSDP
    placed = (
        P(both, None),
        P(None, FSDP),
        P(FSDP),
        P(both, None),
        P(both),
        P(CLIENT, FSDP),
        P(FSDP),
    )
    return jax.shard_map(
        local,
        mesh=split_mesh,
        in_specs=placed,
        out_specs=(P(CLIENT, FSDP), P(FSDP)),
        check_vma=False,
    )
```

```python
import functools
import math

import jax
import jax.numpy as jnp
from jax import lax
from jax.experimental import pallas as pl
from jax.experimental.pallas import tpu as pltpu
from jax.sharding import Mesh, PartitionSpec as P

D = 4608
HD = 2048
epsilon = 1e-06
CLIENT = ("xh", "z", "core")
FSDP = ("y", "xl")
BOUND = math.sqrt(HD * D)
f32 = jnp.float32
bf16 = jnp.bfloat16


def swap(x, axis):
    return lax.ppermute(x, axis, [(0, 1), (1, 0)])


def full(shape):
    return pl.BlockSpec(shape, lambda *i: (0,) * len(shape))


def split_kernel(place_ref, own_ref, got_ref, gown_ref, ggot_ref, *rest):
    outs, sum_ref, total = rest[:4], rest[4], rest[5]
    step = pl.program_id(0)
    block = own_ref[...] + got_ref[...]
    squares = block * block
    folded = squares[:, :128] + squares[:, 128:256] + squares[:, 256:384] + squares[:, 384:]

    @pl.when(step == 0)
    def _():
        total[...] = folded

    @pl.when(step > 0)
    def _():
        total[...] += folded

    gain = gown_ref[...] + ggot_ref[...]
    high = gain.astype(bf16).astype(f32)
    extra = jnp.concatenate([high, gain - high, jnp.zeros((10, 128), f32)], axis=0).astype(bf16)
    left = lax.broadcasted_iota(jnp.int32, (144, 128), 1) < 64
    zero = place_ref[1] == 0

    def pack(same, other):
        for i in range(4):
            part = block[:, i * 128 : i * 128 + 128]
            low, up = part[:144], part[144:]
            first = jnp.where(left, low, pltpu.roll(up, 64, 1))
            second = jnp.where(left, pltpu.roll(low, 64, 1), up)
            same[i * 144 : i * 144 + 144] = jnp.where(zero, first, second).astype(bf16)
            other[i * 144 : i * 144 + 144] = jnp.where(zero, second, first).astype(bf16)
        same[576:] = extra
        other[576:] = extra

    @pl.when(step < 2)
    def _():
        pack(outs[0], outs[1])

    @pl.when(step >= 2)
    def _():
        pack(outs[2], outs[3])

    @pl.when(step == 3)
    def _():
        sum_ref[...] = jnp.full((64, 128), jnp.sum(total[...]) + jnp.sum(gain * gain), f32)


def split(place, own, got, gown, ggot):
    block = pl.BlockSpec((288, 512), lambda n, place: (0, (place[0] ^ (n // 2)) * 2 + n % 2))
    near = pl.BlockSpec((592, 128), lambda n, place: (jnp.minimum(n, 1), 0))
    far = pl.BlockSpec((592, 128), lambda n, place: (jnp.maximum(n - 2, 0), 0))
    packed = jax.ShapeDtypeStruct((1184, 128), bf16)
    return pl.pallas_call(
        split_kernel,
        grid_spec=pltpu.PrefetchScalarGridSpec(
            num_scalar_prefetch=1,
            grid=(4,),
            in_specs=[block, block, full((3, 128)), full((3, 128))],
            out_specs=[near, near, far, far, full((64, 128))],
            scratch_shapes=[pltpu.VMEM((288, 128), f32)],
        ),
        out_shape=[packed, packed, packed, packed, jax.ShapeDtypeStruct((64, 128), f32)],
        name="pack_by_owner",
    )(place, own, got, gown, ggot)


def combine_kernel(place_ref, sums_ref, a_ref, b_ref, c_ref, d_ref, out_ref):
    odd = lax.broadcasted_iota(jnp.int32, (32, 128), 0) % 2
    factors = []
    for h in range(2):
        rows = sums_ref[32 * h : 32 * h + 32]
        for p in range(2):
            norm = jnp.sum(jnp.where(odd == p, rows, 0.0), axis=0, keepdims=True)
            factors.append(BOUND / jnp.maximum(jnp.sqrt(norm), BOUND))
    high_zero = place_ref[0] == 0
    core_zero = place_ref[2] == 0
    near = [jnp.where(high_zero, factors[p], factors[2 + p]) for p in range(2)]
    far = [jnp.where(high_zero, factors[2 + p], factors[p]) for p in range(2)]
    weights = []
    for pair in (near, far):
        weights.append(jnp.where(core_zero, pair[0], pair[1]))
        weights.append(jnp.where(core_zero, pair[1], pair[0]))
    refs = (a_ref, b_ref, c_ref, d_ref)

    def weighted(start, size):
        total = weights[0] * refs[0][start : start + size].astype(f32)
        for w, ref in zip(weights[1:], refs[1:]):
            total = total + w * ref[start : start + size].astype(f32)
        return total

    tail = weighted(576, 16)
    gain = tail[0:3] + tail[3:6]
    high = gain.astype(bf16).astype(f32)
    extra = jnp.concatenate([high, gain - high, jnp.zeros((10, 128), f32)], axis=0).astype(bf16)
    for i in range(4):
        out_ref[i, :144] = weighted(i * 144, 144).astype(bf16)
        out_ref[i, 144:] = extra


def combine(place, sums, parts):
    block = pl.BlockSpec((592, 128), lambda n: (n, 0))
    return pl.pallas_call(
        combine_kernel,
        grid=(2,),
        in_specs=[pl.BlockSpec(memory_space=pltpu.SMEM), full((64, 128))] + [block] * 4,
        out_specs=pl.BlockSpec((4, 160, 128), lambda n: (n, 0, 0)),
        out_shape=jax.ShapeDtypeStruct((8, 160, 128), bf16),
        name="clip_and_combine",
    )(place, sums, *parts)


def finish_kernel(parts_ref, noise_ref, gain_noise_ref, out_ref, gain_ref):
    total = parts_ref[0].astype(f32)
    for i in range(1, 8):
        total = total + parts_ref[i].astype(f32)
    body = total[:144]
    rows = jnp.concatenate([body, pltpu.roll(body, 64, 1)], axis=0).T
    out_ref[...] = (rows[:64] + noise_ref[...]) * (1.0 / 32.0)
    gain_ref[...] = (total[144:147] + total[147:150] + gain_noise_ref[...]) * (1.0 / 32.0)


def finish(parts, noise, gain_noise):
    return pl.pallas_call(
        finish_kernel,
        out_shape=[jax.ShapeDtypeStruct((64, 288), f32), jax.ShapeDtypeStruct((3, 128), f32)],
        name="sum_and_noise",
    )(parts, noise, gain_noise)


def lanes(vector):
    return jnp.pad(vector, (0, 96)).reshape(3, 128)


def turn(x):
    return lax.ppermute(x, ("core", "xl"), [(0, 0), (1, 2), (2, 1), (3, 3)])


def to_owner(x, flip_high, flip_core):
    pairs = []
    for h in range(2):
        for c in range(2):
            for p in range(2):
                pairs.append((h * 4 + c * 2 + p, (h ^ flip_high) * 4 + (p ^ flip_core) * 2 + c))
    return lax.ppermute(x, ("xh", "core", "xl"), pairs)


def local(head_outputs, out_weight, norm_gain, cotangent, loss_mask, weight_noise, gain_noise):
    xl = lax.axis_index("xl")
    core = lax.axis_index("core")
    place = jnp.stack([lax.axis_index("xh"), xl, core]).astype(jnp.int32)
    turned = turn(head_outputs)
    heads = lax.all_gather(turned, "y", axis=0, tiled=True)
    masked = cotangent * loss_mask[:, None].astype(bf16)
    pieces = masked.reshape(128, 8, 2, 288).transpose(1, 2, 3, 0)
    low, high = pieces[:, 0], pieces[:, 1]
    ordered = jnp.concatenate(
        [jnp.where(xl == 0, low, high), jnp.where(xl == 0, high, low)], axis=1
    )
    arrived = turn(lax.all_to_all(ordered, "y", split_axis=0, concat_axis=0, tiled=True))
    arrived = arrived.transpose(1, 0, 2).reshape(576, 1024).astype(f32)
    weight_t, own_gain, _ = lax.optimization_barrier((out_weight.T, norm_gain, turned))
    weight_got, gain_got = swap(weight_t, "xl"), swap(own_gain, "xl")
    straight = xl == core
    weights = jnp.concatenate(
        [jnp.where(straight, weight_t, weight_got), jnp.where(straight, weight_got, weight_t)], axis=0
    )
    gain = jnp.concatenate(
        [jnp.where(straight, own_gain, gain_got), jnp.where(straight, gain_got, own_gain)]
    )[:, None]
    projected = lax.dot_general(
        weights, heads, (((1,), (1,)), ((), ())), preferred_element_type=f32
    )
    stats = jnp.stack(
        [jnp.sum(projected * projected, axis=0), jnp.sum(projected * gain * arrived, axis=0)]
    )
    stats = jnp.sum(
        lax.all_to_all(
            jnp.broadcast_to(stats[None], (8, 2, 1024)), "y", split_axis=0, concat_axis=0, tiled=True
        ),
        axis=0,
    )
    inverse = lax.rsqrt(stats[0:1] / D + epsilon)
    products = stats[1:2]
    back_grad = (
        inverse * gain * arrived - projected * (inverse * inverse * inverse * products / D)
    ).astype(bf16)
    contract = (((1,), (0,)), ((), ()))
    other_part = lax.dot_general(back_grad[288:], heads, contract, preferred_element_type=f32)
    got_part = swap(other_part, "core")
    own_part = lax.dot_general(back_grad[:288], heads, contract, preferred_element_type=f32)
    gain_part = jnp.sum(arrived * projected * inverse, axis=1)
    gain_got = swap(lanes(gain_part[288:]), "core")
    *packed, squares = split(place, own_part, got_part, lanes(gain_part[:288]), gain_got)
    parts = [to_owner(packed[i], i // 2, i % 2) for i in range(4)]
    sums = lax.all_to_all(squares, ("xh", "core", "y", "xl"), split_axis=0, concat_axis=0, tiled=True)
    chip = combine(place, sums, parts)
    over_z = lax.all_to_all(chip, "z", split_axis=0, concat_axis=0, tiled=True)
    update, gain_update = finish(over_z, weight_noise, lanes(gain_noise))
    return update, gain_update.reshape(384)[:288]


def solution(mesh):
    split_mesh = Mesh(mesh.devices.reshape(2, 8, 2, 8, 2), CLIENT + FSDP)
    both = CLIENT + FSDP
    placed = (
        P(both, None),
        P(None, FSDP),
        P(FSDP),
        P(both, None),
        P(both),
        P(CLIENT, FSDP),
        P(FSDP),
    )
    return jax.shard_map(
        local,
        mesh=split_mesh,
        in_specs=placed,
        out_specs=(P(CLIENT, FSDP), P(FSDP)),
        check_vma=False,
    )
```

```python
import functools
import math

import jax
import jax.numpy as jnp
from jax import lax
from jax.experimental import pallas as pl
from jax.experimental.pallas import tpu as pltpu
from jax.sharding import Mesh, PartitionSpec as P

D = 4608
HD = 2048
epsilon = 1e-06
CLIENT = ("xh", "z", "core")
FSDP = ("y", "xl")
BOUND = math.sqrt(HD * D)
f32 = jnp.float32
bf16 = jnp.bfloat16


def swap(x, axis):
    return lax.ppermute(x, axis, [(0, 1), (1, 0)])


def full(shape):
    return pl.BlockSpec(shape, lambda *i: (0,) * len(shape))


def place_spec():
    return pl.BlockSpec(memory_space=pltpu.SMEM)


def whole():
    return pl.BlockSpec(memory_space=pltpu.VMEM)


def project_kernel(wa_ref, wb_ref, gain_ref, heads_ref, masked_ref, out_ref, stats_ref):
    squares = jnp.zeros((1, 256), f32)
    products = jnp.zeros((1, 256), f32)
    for i, w_ref in enumerate((wa_ref, wb_ref)):
        rows = slice(288 * i, 288 * i + 288)
        p = lax.dot_general(
            w_ref[...], heads_ref[...], (((1,), (1,)), ((), ())), preferred_element_type=f32
        )
        out_ref[rows] = p
        squares += jnp.sum(p * p, axis=0, keepdims=True)
        scaled = p * gain_ref[rows]
        masked = jnp.concatenate([masked_ref[0, rows], masked_ref[1, rows]], axis=1).astype(f32)
        products += jnp.sum(scaled * masked, axis=0, keepdims=True)
    both = jnp.concatenate([squares, products], axis=0)
    for i in range(8):
        stats_ref[i] = both


def project(wa, wb, gain, heads, masked):
    return pl.pallas_call(
        project_kernel,
        grid=(4,),
        in_specs=[
            whole(),
            whole(),
            whole(),
            pl.BlockSpec((256, 2048), lambda n: (n, 0)),
            pl.BlockSpec((2, 576, 128), lambda n: (n, 0, 0)),
        ],
        out_specs=[
            pl.BlockSpec((576, 256), lambda n: (0, n)),
            pl.BlockSpec((8, 2, 256), lambda n: (0, 0, n)),
        ],
        out_shape=[jax.ShapeDtypeStruct((576, 1024), f32), jax.ShapeDtypeStruct((8, 2, 1024), f32)],
        cost_estimate=pl.CostEstimate(flops=2 * 576 * 1024 * 2048, bytes_accessed=12000000, transcendentals=0),
        compiler_params=pltpu.CompilerParams(vmem_limit_bytes=50 * 2**20),
        name="project",
    )(wa, wb, gain, heads, masked)


def grad_kernel(place_ref, proj_ref, masked_ref, gain_ref, stats_ref, heads_ref, send_ref, keep_ref, other_ref, gain_keep_ref):
    @pl.when(pl.program_id(0) == 0)
    def _():
        stats = stats_ref[0]
        for i in range(1, 8):
            stats = stats + stats_ref[i]
        inverse = lax.rsqrt(stats[0:1] / D + epsilon)
        coefficient = inverse * inverse * inverse * stats[1:2] / D
        gains = []
        for half, out in enumerate((keep_ref, other_ref)):
            rows = slice(288 * half, 288 * half + 288)
            gain = gain_ref[rows]
            total = jnp.zeros((288, 128), f32)
            for i in range(8):
                lane = slice(128 * i, 128 * i + 128)
                p = proj_ref[rows, lane]
                m = masked_ref[i, rows].astype(f32) * inverse[:, lane]
                out[:, lane] = (gain * m - p * coefficient[:, lane]).astype(bf16)
                total += m * p
            row = jnp.sum(total.T, axis=0, keepdims=True)
            row = jnp.concatenate([row, jnp.zeros((1, 96), f32)], axis=1)
            gains.append([row[:, 0:128], row[:, 128:256], row[:, 256:384]])
        gain_keep_ref[...] = jnp.concatenate(gains[0], axis=0)
        send_ref[288:, :128] = jnp.concatenate(gains[1] + [jnp.zeros((5, 128), f32)], axis=0)

    send_ref[:288] = jnp.dot(other_ref[...], heads_ref[...], preferred_element_type=f32)


def near_columns(first):
    return pl.BlockSpec((1024, 512), lambda n, place: (0, (place[0] ^ first) * 2 + n))


def gradients(place, projected, masked, gain, stats, heads):
    fixed = lambda shape: pl.BlockSpec(shape, lambda n, place: (0,) * len(shape))
    half = jax.ShapeDtypeStruct((288, 1024), bf16)
    return pl.pallas_call(
        grad_kernel,
        grid_spec=pltpu.PrefetchScalarGridSpec(
            num_scalar_prefetch=1,
            grid=(2,),
            in_specs=[whole(), whole(), whole(), whole(), near_columns(0)],
            out_specs=[
                pl.BlockSpec((296, 512), lambda n, place: (0, n)),
                fixed((288, 1024)),
                fixed((288, 1024)),
                fixed((3, 128)),
            ],
        ),
        out_shape=[
            jax.ShapeDtypeStruct((296, 1024), f32),
            half,
            half,
            jax.ShapeDtypeStruct((3, 128), f32),
        ],
        cost_estimate=pl.CostEstimate(flops=2 * 288 * 1024 * 1024, bytes_accessed=8000000, transcendentals=0),
        name="gradients",
    )(place, projected, masked, gain, stats, heads)


def delta_kernel(place_ref, grad_ref, heads_ref, out_ref):
    out_ref[...] = jnp.dot(grad_ref[...], heads_ref[...], preferred_element_type=f32)


def delta(place, grad, heads, far):
    return pl.pallas_call(
        delta_kernel,
        grid_spec=pltpu.PrefetchScalarGridSpec(
            num_scalar_prefetch=1,
            grid=(2,),
            in_specs=[whole(), near_columns(far)],
            out_specs=pl.BlockSpec((288, 512), lambda n, place: (0, n)),
        ),
        out_shape=jax.ShapeDtypeStruct((288, 1024), f32),
        cost_estimate=pl.CostEstimate(flops=2 * 288 * 1024 * 1024, bytes_accessed=4000000, transcendentals=0),
        name="delta",
    )(place, grad, heads)


def pack_rows(place_ref, own_ref, got_ref, extra, same, other, total=None):
    left = lax.broadcasted_iota(jnp.int32, (144, 128), 1) < 64
    zero = place_ref[1] == 0
    for i in range(8):
        lane = slice(i * 128, i * 128 + 128)
        part = own_ref[:, lane] + got_ref[:288, lane]
        if total is not None:
            total = total + part * part
        low, up = part[:144], part[144:]
        first = jnp.where(left, low, pltpu.roll(up, 64, 1))
        second = jnp.where(left, pltpu.roll(low, 64, 1), up)
        rows = slice(i * 144, i * 144 + 144)
        same[rows] = jnp.where(zero, first, second).astype(bf16)
        other[rows] = jnp.where(zero, second, first).astype(bf16)
    same[1152:] = extra
    other[1152:] = extra
    return total


def near_kernel(place_ref, own_ref, got_ref, gain_ref, same_ref, other_ref, sum_ref, gain_out_ref, extra_ref):
    gain = gain_ref[...] + got_ref[288:291, :128]
    high = gain.astype(bf16).astype(f32)
    extra = jnp.concatenate([high, gain - high, jnp.zeros((10, 128), f32)], axis=0).astype(bf16)
    total = pack_rows(place_ref, own_ref, got_ref, extra, same_ref, other_ref, jnp.zeros((288, 128), f32))
    sum_ref[...] = jnp.sum(total, axis=0, keepdims=True)
    gain_out_ref[...] = gain
    extra_ref[...] = extra


packed = jax.ShapeDtypeStruct((1168, 128), bf16)


def pack_near(place, own, got, gain):
    return pl.pallas_call(
        near_kernel,
        in_specs=[place_spec(), whole(), whole(), whole()],
        out_specs=[whole()] * 5,
        out_shape=[
            packed,
            packed,
            jax.ShapeDtypeStruct((1, 128), f32),
            jax.ShapeDtypeStruct((3, 128), f32),
            jax.ShapeDtypeStruct((16, 128), bf16),
        ],
        cost_estimate=pl.CostEstimate(flops=4000000, bytes_accessed=10000000, transcendentals=0),
        name="pack_near_rows",
    )(place, own, got, gain)


def far_kernel(place_ref, own_ref, got_ref, extra_ref, squared_ref, same_ref, other_ref):
    pack_rows(place_ref, own_ref, got_ref, extra_ref[...], same_ref, other_ref)


def pack_far(place, own, got, extra, squared):
    return pl.pallas_call(
        far_kernel,
        in_specs=[place_spec(), whole(), whole(), whole(), whole()],
        out_specs=[whole()] * 2,
        out_shape=[packed, packed],
        cost_estimate=pl.CostEstimate(flops=4000000, bytes_accessed=10000000, transcendentals=0),
        name="pack_far_rows",
    )(place, own, got, extra, squared)


def squares_kernel(own_ref, got_ref, near_ref, gain_ref, out_ref):
    total = jnp.zeros((288, 128), f32)
    for i in range(8):
        lane = slice(i * 128, i * 128 + 128)
        part = own_ref[:, lane] + got_ref[:, lane]
        total = total + part * part
    gain = gain_ref[...]
    out_ref[...] = jnp.full((64, 8, 128), jnp.sum(total) + jnp.sum(near_ref[...]) + jnp.sum(gain * gain), f32)


def squares(own, got, near, gain):
    return pl.pallas_call(
        squares_kernel,
        in_specs=[whole()] * 4,
        out_specs=whole(),
        out_shape=jax.ShapeDtypeStruct((64, 8, 128), f32),
        name="sum_of_squares",
    )(own, got, near, gain)


def combine_kernel(place_ref, sums_ref, a_ref, b_ref, c_ref, d_ref, out_ref):
    odd = lax.broadcasted_iota(jnp.int32, (32, 128), 0) % 2
    factors = []
    for h in range(2):
        rows = sums_ref[32 * h : 32 * h + 32, 0]
        for p in range(2):
            norm = jnp.sum(jnp.where(odd == p, rows, 0.0), axis=0, keepdims=True)
            factors.append(BOUND / jnp.maximum(jnp.sqrt(norm), BOUND))
    high_zero = place_ref[0] == 0
    core_zero = place_ref[2] == 0
    near = [jnp.where(high_zero, factors[p], factors[2 + p]) for p in range(2)]
    far = [jnp.where(high_zero, factors[2 + p], factors[p]) for p in range(2)]
    weights = []
    for pair in (near, far):
        weights.append(jnp.where(core_zero, pair[0], pair[1]))
        weights.append(jnp.where(core_zero, pair[1], pair[0]))
    refs = (a_ref, b_ref, c_ref, d_ref)

    def weighted(start, size):
        total = weights[0] * refs[0][start : start + size].astype(f32)
        for w, ref in zip(weights[1:], refs[1:]):
            total = total + w * ref[start : start + size].astype(f32)
        return total

    tail = weighted(1152, 16)
    gain = tail[0:3] + tail[3:6]
    high = gain.astype(bf16).astype(f32)
    extra = jnp.concatenate([high, gain - high, jnp.zeros((10, 128), f32)], axis=0).astype(bf16)
    for i in range(8):
        out_ref[i, :144] = weighted(i * 144, 144).astype(bf16)
        out_ref[i, 144:] = extra


def combine(place, sums, parts):
    return pl.pallas_call(
        combine_kernel,
        in_specs=[place_spec()] + [whole()] * 5,
        out_specs=whole(),
        out_shape=jax.ShapeDtypeStruct((8, 160, 128), bf16),
        name="clip_and_combine",
    )(place, sums, *parts)


def finish_kernel(parts_ref, noise_ref, gain_noise_ref, out_ref, gain_ref):
    total = parts_ref[0].astype(f32)
    for i in range(1, 8):
        total = total + parts_ref[i].astype(f32)
    body = total[:144]
    rows = jnp.concatenate([body, pltpu.roll(body, 64, 1)], axis=0).T
    out_ref[...] = (rows[:64] + noise_ref[...]) * (1.0 / 32.0)
    gain_ref[...] = (total[144:147] + total[147:150] + gain_noise_ref[...]) * (1.0 / 32.0)


def finish(parts, noise, gain_noise):
    return pl.pallas_call(
        finish_kernel,
        out_shape=[jax.ShapeDtypeStruct((64, 288), f32), jax.ShapeDtypeStruct((3, 128), f32)],
        name="sum_and_noise",
    )(parts, noise, gain_noise)


def lanes(vector):
    return jnp.pad(vector, (0, 96)).reshape(3, 128)


def turn(x):
    return lax.ppermute(x, ("core", "xl"), [(0, 0), (1, 2), (2, 1), (3, 3)])


def to_owner(x, flip_high, flip_core):
    pairs = []
    for h in range(2):
        for c in range(2):
            for p in range(2):
                pairs.append((h * 4 + c * 2 + p, (h ^ flip_high) * 4 + (p ^ flip_core) * 2 + c))
    return lax.ppermute(x, ("xh", "core", "xl"), pairs)


def local(head_outputs, out_weight, norm_gain, cotangent, loss_mask, weight_noise, gain_noise):
    xl = lax.axis_index("xl")
    core = lax.axis_index("core")
    place = jnp.stack([lax.axis_index("xh"), xl, core]).astype(jnp.int32)
    masked = cotangent * loss_mask[:, None].astype(bf16)
    pieces = masked.reshape(128, 8, 2, 288).transpose(1, 2, 3, 0)
    low, high = pieces[:, 0], pieces[:, 1]
    ordered = jnp.concatenate(
        [jnp.where(xl == 0, low, high), jnp.where(xl == 0, high, low)], axis=1
    )
    ordered, turned = lax.optimization_barrier((ordered, turn(head_outputs)))
    heads = lax.all_gather(turned, "y", axis=0, tiled=True)
    arrived = turn(lax.all_to_all(ordered, "y", split_axis=0, concat_axis=0, tiled=True))
    weight_t, own_gain, _ = lax.optimization_barrier((out_weight.T, norm_gain, turned))
    weight_got, gain_got = swap(weight_t, "xl"), swap(own_gain, "xl")
    straight = xl == core
    first_weight = jnp.where(straight, weight_t, weight_got)
    second_weight = jnp.where(straight, weight_got, weight_t)
    gain = jnp.concatenate(
        [jnp.where(straight, own_gain, gain_got), jnp.where(straight, gain_got, own_gain)]
    )[:, None]
    projected, stats = project(first_weight, second_weight, gain, heads, arrived)
    stats = lax.all_to_all(stats, "y", split_axis=0, concat_axis=0, tiled=True)
    send_near, keep_grad, other_grad, gain_keep = gradients(place, projected, arrived, gain, stats, heads)
    got_near = swap(send_near, "core")
    got_far = swap(delta(place, other_grad, heads, 1), "core")
    own_near = delta(place, keep_grad, heads, 0)
    own_far = delta(place, keep_grad, heads, 1)
    same_near, other_near, near_sum, gain_sum, extra = pack_near(place, own_near, got_near, gain_keep)
    squared = squares(own_far, got_far, near_sum, gain_sum)
    sums = lax.all_to_all(squared, ("xh", "core", "y", "xl"), split_axis=0, concat_axis=0, tiled=True)
    parts = [to_owner(same_near, 0, 0), to_owner(other_near, 0, 1)]
    extra, *parts = lax.optimization_barrier((extra, *parts))
    same_far, other_far = pack_far(place, own_far, got_far, extra, squared)
    parts += [to_owner(same_far, 1, 0), to_owner(other_far, 1, 1)]
    chip = combine(place, sums, parts)
    over_z = lax.all_to_all(chip, "z", split_axis=0, concat_axis=0, tiled=True)
    update, gain_update = finish(over_z, weight_noise, lanes(gain_noise))
    return update, gain_update.reshape(384)[:288]


def solution(mesh):
    split_mesh = Mesh(mesh.devices.reshape(2, 8, 2, 8, 2), CLIENT + FSDP)
    both = CLIENT + FSDP
    placed = (
        P(both, None),
        P(None, FSDP),
        P(FSDP),
        P(both, None),
        P(both),
        P(CLIENT, FSDP),
        P(FSDP),
    )
    return jax.shard_map(
        local,
        mesh=split_mesh,
        in_specs=placed,
        out_specs=(P(CLIENT, FSDP), P(FSDP)),
        check_vma=False,
    )
```

```python
import functools
import math

import jax
import jax.numpy as jnp
from jax import lax
from jax.experimental import pallas as pl
from jax.experimental.pallas import tpu as pltpu
from jax.sharding import Mesh, PartitionSpec as P

D = 4608
HD = 2048
epsilon = 1e-06
CLIENT = ("xh", "z", "core")
FSDP = ("y", "xl")
BOUND = math.sqrt(HD * D)
f32 = jnp.float32
bf16 = jnp.bfloat16


def swap(x, axis):
    return lax.ppermute(x, axis, [(0, 1), (1, 0)])


def full(shape):
    return pl.BlockSpec(shape, lambda *i: (0,) * len(shape))


def place_spec():
    return pl.BlockSpec(memory_space=pltpu.SMEM)


def whole():
    return pl.BlockSpec(memory_space=pltpu.VMEM)


def pack_rows(place_ref, own_ref, got_ref, extra, same, other):
    left = lax.broadcasted_iota(jnp.int32, (144, 128), 1) < 64
    zero = place_ref[1] == 0
    total = jnp.zeros((144, 128), f32)
    for i in range(8):
        lane = slice(i * 128, i * 128 + 128)
        part = own_ref[:, lane] + got_ref[:, lane]
        low, up = part[:144], part[144:]
        total = total + low * low + up * up
        first = jnp.where(left, low, pltpu.roll(up, 64, 1))
        second = jnp.where(left, pltpu.roll(low, 64, 1), up)
        rows = slice(i * 144, i * 144 + 144)
        same[rows] = jnp.where(zero, first, second).astype(bf16)
        other[rows] = jnp.where(zero, second, first).astype(bf16)
    same[1152:] = extra
    other[1152:] = extra
    return total


def gain_rows(gain):
    high = gain.astype(bf16).astype(f32)
    return jnp.concatenate([high, gain - high, jnp.zeros((10, 128), f32)], axis=0).astype(bf16)


def far_kernel(place_ref, own_ref, got_ref, gown_ref, ggot_ref, same_ref, other_ref, sum_ref):
    gain = gown_ref[...] + ggot_ref[...]
    total = pack_rows(place_ref, own_ref, got_ref, gain_rows(gain), same_ref, other_ref)
    sum_ref[...] = jnp.sum(total, axis=0, keepdims=True)


def near_kernel(place_ref, own_ref, got_ref, gown_ref, ggot_ref, far_ref, same_ref, other_ref, sum_ref):
    gain = gown_ref[...] + ggot_ref[...]
    total = pack_rows(place_ref, own_ref, got_ref, gain_rows(gain), same_ref, other_ref)
    total = jnp.sum(total) + jnp.sum(far_ref[...]) + jnp.sum(gain * gain)
    sum_ref[...] = jnp.full(sum_ref.shape, total, f32)


packed = jax.ShapeDtypeStruct((1168, 128), bf16)
COST = pl.CostEstimate(flops=4000000, bytes_accessed=8000000, transcendentals=0)


def pack_far(place, own, got, gown, ggot):
    return pl.pallas_call(
        far_kernel,
        in_specs=[place_spec()] + [whole()] * 4,
        out_specs=[whole()] * 3,
        out_shape=[packed, packed, jax.ShapeDtypeStruct((1, 128), f32)],
        cost_estimate=COST,
        name="pack_far_rows",
    )(place, own, got, gown, ggot)


def pack_near(place, own, got, gown, ggot, far):
    return pl.pallas_call(
        near_kernel,
        in_specs=[place_spec()] + [whole()] * 5,
        out_specs=[whole()] * 3,
        out_shape=[packed, packed, jax.ShapeDtypeStruct((64, 8, 128), f32)],
        cost_estimate=COST,
        name="pack_near_rows",
    )(place, own, got, gown, ggot, far)


def combine_kernel(place_ref, sums_ref, a_ref, b_ref, c_ref, d_ref, out_ref):
    odd = lax.broadcasted_iota(jnp.int32, (32, 128), 0) % 2
    factors = []
    for h in range(2):
        rows = sums_ref[32 * h : 32 * h + 32, 0]
        for p in range(2):
            norm = jnp.sum(jnp.where(odd == p, rows, 0.0), axis=0, keepdims=True)
            factors.append(BOUND / jnp.maximum(jnp.sqrt(norm), BOUND))
    high_zero = place_ref[0] == 0
    core_zero = place_ref[2] == 0
    near = [jnp.where(high_zero, factors[p], factors[2 + p]) for p in range(2)]
    far = [jnp.where(high_zero, factors[2 + p], factors[p]) for p in range(2)]
    weights = []
    for pair in (far, near):
        weights.append(jnp.where(core_zero, pair[0], pair[1]))
        weights.append(jnp.where(core_zero, pair[1], pair[0]))
    refs = (a_ref, b_ref, c_ref, d_ref)

    def weighted(start, size):
        total = weights[0] * refs[0][start : start + size].astype(f32)
        for w, ref in zip(weights[1:], refs[1:]):
            total = total + w * ref[start : start + size].astype(f32)
        return total

    tail = weighted(1152, 16)
    gain = tail[0:3] + tail[3:6]
    high = gain.astype(bf16).astype(f32)
    extra = jnp.concatenate([high, gain - high, jnp.zeros((10, 128), f32)], axis=0).astype(bf16)
    for i in range(8):
        out_ref[i, :144] = weighted(i * 144, 144).astype(bf16)
        out_ref[i, 144:] = extra


def combine(place, sums, parts):
    return pl.pallas_call(
        combine_kernel,
        in_specs=[place_spec()] + [whole()] * 5,
        out_specs=whole(),
        out_shape=jax.ShapeDtypeStruct((8, 160, 128), bf16),
        name="clip_and_combine",
    )(place, sums, *parts)


def finish_kernel(parts_ref, noise_ref, gain_noise_ref, out_ref, gain_ref):
    total = parts_ref[0].astype(f32)
    for i in range(1, 8):
        total = total + parts_ref[i].astype(f32)
    body = total[:144]
    rows = jnp.concatenate([body, pltpu.roll(body, 64, 1)], axis=0).T
    out_ref[...] = (rows[:64] + noise_ref[...]) * (1.0 / 32.0)
    gain_ref[...] = (total[144:147] + total[147:150] + gain_noise_ref[...]) * (1.0 / 32.0)


def finish(parts, noise, gain_noise):
    return pl.pallas_call(
        finish_kernel,
        out_shape=[jax.ShapeDtypeStruct((64, 288), f32), jax.ShapeDtypeStruct((3, 128), f32)],
        name="sum_and_noise",
    )(parts, noise, gain_noise)


def lanes(vector):
    return jnp.pad(vector, (0, 96)).reshape(3, 128)


def turn(x):
    return lax.ppermute(x, ("core", "xl"), [(0, 0), (1, 2), (2, 1), (3, 3)])


def to_owner(x, flip_high, flip_core):
    pairs = []
    for h in range(2):
        for c in range(2):
            for p in range(2):
                pairs.append((h * 4 + c * 2 + p, (h ^ flip_high) * 4 + (p ^ flip_core) * 2 + c))
    return lax.ppermute(x, ("xh", "core", "xl"), pairs)


def far_first(high_zero, x):
    low, high = x[:, :1024], x[:, 1024:]
    return jnp.where(high_zero, jnp.concatenate([high, low], axis=1), x)


def local(head_outputs, out_weight, norm_gain, cotangent, loss_mask, weight_noise, gain_noise):
    xl = lax.axis_index("xl")
    core = lax.axis_index("core")
    place = jnp.stack([lax.axis_index("xh"), xl, core]).astype(jnp.int32)
    high_zero = lax.axis_index("xh") == 0
    turned = turn(far_first(high_zero, head_outputs))
    heads = lax.all_gather(turned, "y", axis=0, tiled=True)
    masked = cotangent * loss_mask[:, None].astype(bf16)
    pieces = masked.reshape(128, 8, 2, 288).transpose(1, 2, 3, 0)
    low, high = pieces[:, 0], pieces[:, 1]
    ordered = jnp.concatenate(
        [jnp.where(xl == 0, low, high), jnp.where(xl == 0, high, low)], axis=1
    )
    arrived = turn(lax.all_to_all(ordered, "y", split_axis=0, concat_axis=0, tiled=True))
    arrived = arrived.transpose(1, 0, 2).reshape(576, 1024).astype(f32)
    weight_t, own_gain, _ = lax.optimization_barrier((out_weight.T, norm_gain, turned))
    weight_t = far_first(high_zero, weight_t)
    weight_got, gain_got = swap(weight_t, "xl"), swap(own_gain, "xl")
    straight = xl == core
    weights = jnp.concatenate(
        [jnp.where(straight, weight_t, weight_got), jnp.where(straight, weight_got, weight_t)], axis=0
    )
    gain = jnp.concatenate(
        [jnp.where(straight, own_gain, gain_got), jnp.where(straight, gain_got, own_gain)]
    )[:, None]
    projected = lax.dot_general(
        weights, heads, (((1,), (1,)), ((), ())), preferred_element_type=f32
    )
    stats = jnp.stack(
        [jnp.sum(projected * projected, axis=0), jnp.sum(projected * gain * arrived, axis=0)]
    )
    stats = jnp.sum(
        lax.all_to_all(
            jnp.broadcast_to(stats[None], (8, 2, 1024)), "y", split_axis=0, concat_axis=0, tiled=True
        ),
        axis=0,
    )
    inverse = lax.rsqrt(stats[0:1] / D + epsilon)
    products = stats[1:2]
    back_grad = (
        inverse * gain * arrived - projected * (inverse * inverse * inverse * products / D)
    ).astype(bf16)
    contract = (((1,), (0,)), ((), ()))
    own_grad, other_grad = back_grad[:288], back_grad[288:]
    far, near = heads[:, :1024], heads[:, 1024:]

    def delta(grad, rows):
        return lax.dot_general(grad, rows, contract, preferred_element_type=f32)

    got_far = swap(delta(other_grad, far), "core")
    got_near = swap(delta(other_grad, near), "core")
    gain_part = jnp.sum(arrived * projected * inverse, axis=1)
    gain_own, gain_got = lanes(gain_part[:288]), swap(lanes(gain_part[288:]), "core")
    same_far, other_far, far_sum = pack_far(place, delta(own_grad, far), got_far, gain_own, gain_got)
    same_near, other_near, squares = pack_near(place, delta(own_grad, near), got_near, gain_own, gain_got, far_sum)
    parts = [
        to_owner(same_far, 1, 0),
        to_owner(other_far, 1, 1),
        to_owner(same_near, 0, 0),
        to_owner(other_near, 0, 1),
    ]
    sums = lax.all_to_all(squares, ("xh", "core", "y", "xl"), split_axis=0, concat_axis=0, tiled=True)
    chip = combine(place, sums, parts)
    over_z = lax.all_to_all(chip, "z", split_axis=0, concat_axis=0, tiled=True)
    update, gain_update = finish(over_z, weight_noise, lanes(gain_noise))
    return update, gain_update.reshape(384)[:288]


def solution(mesh):
    split_mesh = Mesh(mesh.devices.reshape(2, 8, 2, 8, 2), CLIENT + FSDP)
    both = CLIENT + FSDP
    placed = (
        P(both, None),
        P(None, FSDP),
        P(FSDP),
        P(both, None),
        P(both),
        P(CLIENT, FSDP),
        P(FSDP),
    )
    return jax.shard_map(
        local,
        mesh=split_mesh,
        in_specs=placed,
        out_specs=(P(CLIENT, FSDP), P(FSDP)),
        check_vma=False,
    )
```

```python
import functools
import math

import jax
import jax.numpy as jnp
from jax import lax
from jax.experimental import pallas as pl
from jax.experimental.pallas import tpu as pltpu
from jax.sharding import Mesh, PartitionSpec as P

D = 4608
HD = 2048
epsilon = 1e-06
CLIENT = ("xh", "z", "core")
FSDP = ("y", "xl")
BOUND = math.sqrt(HD * D)
f32 = jnp.float32
bf16 = jnp.bfloat16


def swap(x, axis):
    return lax.ppermute(x, axis, [(0, 1), (1, 0)])


def full(shape):
    return pl.BlockSpec(shape, lambda *i: (0,) * len(shape))


def place_spec():
    return pl.BlockSpec(memory_space=pltpu.SMEM)


def whole():
    return pl.BlockSpec(memory_space=pltpu.VMEM)


SLOTS = ((1, 0), (0, 1), (0, 0), (1, 1))


def regroup(high, flip, src, dst):
    left = lax.broadcasted_iota(jnp.int32, (src.shape[0], 128), 1) < 64
    for d in range(2):
        for j in range(4):
            base = ((high ^ d) * 8 + 2 * j) * 128
            a = src[:, pl.ds(pl.multiple_of(base, 128), 128)].astype(f32)
            b = src[:, pl.ds(pl.multiple_of(base + 128, 128), 128)].astype(f32)
            first = jnp.where(left, a, pltpu.roll(b, 64, 1))
            second = jnp.where(left, pltpu.roll(a, 64, 1), b)
            same, other = SLOTS.index((d, 0)) * 512 + j * 128, SLOTS.index((d, 1)) * 512 + j * 128
            dst[:, same : same + 128] = jnp.where(flip == 0, first, second).astype(bf16)
            dst[:, other : other + 128] = jnp.where(flip == 0, second, first).astype(bf16)


def heads_kernel(place_ref, heads_ref, out_ref):
    regroup(place_ref[0], place_ref[2], heads_ref, out_ref)


def order_heads(place, heads):
    return pl.pallas_call(
        heads_kernel,
        in_specs=[place_spec(), whole()],
        out_specs=whole(),
        out_shape=jax.ShapeDtypeStruct((128, 2048), bf16),
        name="order_heads",
    )(place, heads)


def weights_kernel(place_ref, own_ref, got_ref, first_ref, second_ref):
    high, flip = place_ref[0], place_ref[1]

    @pl.when(flip == place_ref[2])
    def _():
        regroup(high, flip, own_ref, first_ref)
        regroup(high, flip, got_ref, second_ref)

    @pl.when(flip != place_ref[2])
    def _():
        regroup(high, flip, got_ref, first_ref)
        regroup(high, flip, own_ref, second_ref)


def order_weights(place, own, got):
    return pl.pallas_call(
        weights_kernel,
        in_specs=[place_spec(), whole(), whole()],
        out_specs=[whole()] * 2,
        out_shape=[jax.ShapeDtypeStruct((288, 2048), bf16)] * 2,
        cost_estimate=pl.CostEstimate(flops=4000000, bytes_accessed=6000000, transcendentals=0),
        name="order_weights",
    )(place, own, got)


def pack(own_ref, got_ref, gown_ref, ggot_ref, refs):
    gain = gown_ref[...] + ggot_ref[...]
    high = gain.astype(bf16).astype(f32)
    extra = jnp.concatenate([high, gain - high, jnp.zeros((10, 128), f32)], axis=0).astype(bf16)
    total = jnp.zeros((288, 128), f32)
    for i in range(8):
        lane = slice(i * 128, i * 128 + 128)
        part = own_ref[:, lane] + got_ref[:, lane]
        total = total + part * part
        out = refs[i // 4]
        lane = slice(i % 4 * 128, i % 4 * 128 + 128)
        out[:288, lane] = part.astype(bf16)
        out[288:, lane] = extra
    return total, gain


def first_kernel(own_ref, got_ref, gown_ref, ggot_ref, a_ref, b_ref, sum_ref):
    total, _ = pack(own_ref, got_ref, gown_ref, ggot_ref, (a_ref, b_ref))
    sum_ref[...] = jnp.sum(total, axis=0, keepdims=True)


def second_kernel(own_ref, got_ref, gown_ref, ggot_ref, first_ref, a_ref, b_ref, sum_ref):
    total, gain = pack(own_ref, got_ref, gown_ref, ggot_ref, (a_ref, b_ref))
    total = jnp.sum(total) + jnp.sum(first_ref[...]) + jnp.sum(gain * gain)
    sum_ref[...] = jnp.full(sum_ref.shape, total, f32)


packed = jax.ShapeDtypeStruct((304, 512), bf16)
COST = pl.CostEstimate(flops=4000000, bytes_accessed=8000000, transcendentals=0)


def pack_first(own, got, gown, ggot):
    return pl.pallas_call(
        first_kernel,
        in_specs=[whole()] * 4,
        out_specs=[whole()] * 3,
        out_shape=[packed, packed, jax.ShapeDtypeStruct((1, 128), f32)],
        cost_estimate=COST,
        name="pack_first_half",
    )(own, got, gown, ggot)


def pack_second(own, got, gown, ggot, first):
    return pl.pallas_call(
        second_kernel,
        in_specs=[whole()] * 5,
        out_specs=[whole()] * 3,
        out_shape=[packed, packed, jax.ShapeDtypeStruct((64, 8, 128), f32)],
        cost_estimate=COST,
        name="pack_second_half",
    )(own, got, gown, ggot, first)


def combine_kernel(place_ref, sums_ref, a_ref, b_ref, c_ref, d_ref, out_ref):
    odd = lax.broadcasted_iota(jnp.int32, (32, 128), 0) % 2
    factors = []
    for h in range(2):
        rows = sums_ref[32 * h : 32 * h + 32, 0]
        for p in range(2):
            norm = jnp.sum(jnp.where(odd == p, rows, 0.0), axis=0, keepdims=True)
            factors.append(BOUND / jnp.maximum(jnp.sqrt(norm), BOUND))
    high_zero = place_ref[0] == 0
    core_zero = place_ref[2] == 0
    weights = []
    for d, c in SLOTS:
        pair = [jnp.where(high_zero, factors[2 * d + p], factors[2 - 2 * d + p]) for p in range(2)]
        weights.append(jnp.where(core_zero, pair[c], pair[1 - c]))
    refs = (a_ref, b_ref, c_ref, d_ref)

    def weighted(rows, lane):
        total = weights[0] * refs[0][rows, lane].astype(f32)
        for w, ref in zip(weights[1:], refs[1:]):
            total = total + w * ref[rows, lane].astype(f32)
        return total

    tail = weighted(slice(288, 304), slice(0, 128))
    gain = tail[0:3] + tail[3:6]
    high = gain.astype(bf16).astype(f32)
    extra = jnp.concatenate([high, gain - high, jnp.zeros((10, 128), f32)], axis=0).astype(bf16)
    left = lax.broadcasted_iota(jnp.int32, (144, 128), 1) < 64
    for j in range(4):
        part = weighted(slice(0, 288), slice(j * 128, j * 128 + 128))
        low, up = part[:144], part[144:]
        out_ref[2 * j, :144] = jnp.where(left, low, pltpu.roll(up, 64, 1)).astype(bf16)
        out_ref[2 * j + 1, :144] = jnp.where(left, pltpu.roll(low, 64, 1), up).astype(bf16)
        out_ref[2 * j, 144:] = extra
        out_ref[2 * j + 1, 144:] = extra


def combine(place, sums, parts):
    return pl.pallas_call(
        combine_kernel,
        in_specs=[place_spec()] + [whole()] * 5,
        out_specs=whole(),
        out_shape=jax.ShapeDtypeStruct((8, 160, 128), bf16),
        name="clip_and_combine",
    )(place, sums, *parts)


def finish_kernel(parts_ref, noise_ref, gain_noise_ref, out_ref, gain_ref):
    total = parts_ref[0].astype(f32)
    for i in range(1, 8):
        total = total + parts_ref[i].astype(f32)
    body = total[:144]
    rows = jnp.concatenate([body, pltpu.roll(body, 64, 1)], axis=0).T
    out_ref[...] = (rows[:64] + noise_ref[...]) * (1.0 / 32.0)
    gain_ref[...] = (total[144:147] + total[147:150] + gain_noise_ref[...]) * (1.0 / 32.0)


def finish(parts, noise, gain_noise):
    return pl.pallas_call(
        finish_kernel,
        out_shape=[jax.ShapeDtypeStruct((64, 288), f32), jax.ShapeDtypeStruct((3, 128), f32)],
        name="sum_and_noise",
    )(parts, noise, gain_noise)


def lanes(vector):
    return jnp.pad(vector, (0, 96)).reshape(3, 128)


def turn(x):
    return lax.ppermute(x, ("core", "xl"), [(0, 0), (1, 2), (2, 1), (3, 3)])


def to_owner(x, flip_high, flip_core):
    pairs = []
    for h in range(2):
        for c in range(2):
            for p in range(2):
                pairs.append((h * 4 + c * 2 + p, (h ^ flip_high) * 4 + (p ^ flip_core) * 2 + c))
    return lax.ppermute(x, ("xh", "core", "xl"), pairs)


def local(head_outputs, out_weight, norm_gain, cotangent, loss_mask, weight_noise, gain_noise):
    xl = lax.axis_index("xl")
    core = lax.axis_index("core")
    place = jnp.stack([lax.axis_index("xh"), xl, core]).astype(jnp.int32)
    turned = turn(order_heads(place, head_outputs))
    heads = lax.all_gather(turned, "y", axis=0, tiled=True)
    masked = cotangent * loss_mask[:, None].astype(bf16)
    pieces = masked.reshape(128, 8, 2, 288).transpose(1, 2, 3, 0)
    low, high = pieces[:, 0], pieces[:, 1]
    ordered = jnp.concatenate(
        [jnp.where(xl == 0, low, high), jnp.where(xl == 0, high, low)], axis=1
    )
    arrived = turn(lax.all_to_all(ordered, "y", split_axis=0, concat_axis=0, tiled=True))
    arrived = arrived.transpose(1, 0, 2).reshape(576, 1024).astype(f32)
    weight_t, own_gain, _ = lax.optimization_barrier((out_weight.T, norm_gain, turned))
    weight_got, gain_got = swap(weight_t, "xl"), swap(own_gain, "xl")
    straight = xl == core
    weights = jnp.concatenate(order_weights(place, weight_t, weight_got), axis=0)
    gain = jnp.concatenate(
        [jnp.where(straight, own_gain, gain_got), jnp.where(straight, gain_got, own_gain)]
    )[:, None]
    projected = lax.dot_general(
        weights, heads, (((1,), (1,)), ((), ())), preferred_element_type=f32
    )
    stats = jnp.stack(
        [jnp.sum(projected * projected, axis=0), jnp.sum(projected * gain * arrived, axis=0)]
    )
    stats = jnp.sum(
        lax.all_to_all(
            jnp.broadcast_to(stats[None], (8, 2, 1024)), "y", split_axis=0, concat_axis=0, tiled=True
        ),
        axis=0,
    )
    inverse = lax.rsqrt(stats[0:1] / D + epsilon)
    products = stats[1:2]
    back_grad = (
        inverse * gain * arrived - projected * (inverse * inverse * inverse * products / D)
    ).astype(bf16)
    contract = (((1,), (0,)), ((), ()))
    own_grad, other_grad = back_grad[:288], back_grad[288:]
    first, second = heads[:, :1024], heads[:, 1024:]

    def delta(grad, columns):
        return lax.dot_general(grad, columns, contract, preferred_element_type=f32)

    got_first = swap(delta(other_grad, first), "core")
    got_second = swap(delta(other_grad, second), "core")
    gain_part = jnp.sum(arrived * projected * inverse, axis=1)
    gain_own, gain_got = lanes(gain_part[:288]), swap(lanes(gain_part[288:]), "core")
    a, b, first_sum = pack_first(delta(own_grad, first), got_first, gain_own, gain_got)
    c, d, squares = pack_second(delta(own_grad, second), got_second, gain_own, gain_got, first_sum)
    a, b = to_owner(a, *SLOTS[0]), to_owner(b, *SLOTS[1])
    a, b, c, d = lax.optimization_barrier((a, b, c, d))
    parts = [a, b, to_owner(c, *SLOTS[2]), to_owner(d, *SLOTS[3])]
    sums = lax.all_to_all(squares, ("xh", "core", "y", "xl"), split_axis=0, concat_axis=0, tiled=True)
    chip = combine(place, sums, parts)
    over_z = lax.all_to_all(chip, "z", split_axis=0, concat_axis=0, tiled=True)
    update, gain_update = finish(over_z, weight_noise, lanes(gain_noise))
    return update, gain_update.reshape(384)[:288]


def solution(mesh):
    split_mesh = Mesh(mesh.devices.reshape(2, 8, 2, 8, 2), CLIENT + FSDP)
    both = CLIENT + FSDP
    placed = (
        P(both, None),
        P(None, FSDP),
        P(FSDP),
        P(both, None),
        P(both),
        P(CLIENT, FSDP),
        P(FSDP),
    )
    return jax.shard_map(
        local,
        mesh=split_mesh,
        in_specs=placed,
        out_specs=(P(CLIENT, FSDP), P(FSDP)),
        check_vma=False,
    )
```

```python
import functools
import math

import jax
import jax.numpy as jnp
from jax import lax
from jax.experimental import pallas as pl
from jax.experimental.pallas import tpu as pltpu
from jax.sharding import Mesh, PartitionSpec as P

D = 4608
HD = 2048
epsilon = 1e-06
CLIENT = ("xh", "z", "core")
FSDP = ("y", "xl")
BOUND = math.sqrt(HD * D)
f32 = jnp.float32
bf16 = jnp.bfloat16


def swap(x, axis):
    return lax.ppermute(x, axis, [(0, 1), (1, 0)])


def full(shape):
    return pl.BlockSpec(shape, lambda *i: (0,) * len(shape))


def place_spec():
    return pl.BlockSpec(memory_space=pltpu.SMEM)


def whole():
    return pl.BlockSpec(memory_space=pltpu.VMEM)


SLOTS = ((1, 0), (0, 1), (0, 0), (1, 1))


def regroup(high, flip, src, dst):
    left = lax.broadcasted_iota(jnp.int32, (src.shape[0], 128), 1) < 64
    for d in range(2):
        for j in range(4):
            base = ((high ^ d) * 8 + 2 * j) * 128
            a = src[:, pl.ds(pl.multiple_of(base, 128), 128)].astype(f32)
            b = src[:, pl.ds(pl.multiple_of(base + 128, 128), 128)].astype(f32)
            first = jnp.where(left, a, pltpu.roll(b, 64, 1))
            second = jnp.where(left, pltpu.roll(a, 64, 1), b)
            same, other = SLOTS.index((d, 0)) * 512 + j * 128, SLOTS.index((d, 1)) * 512 + j * 128
            dst[:, same : same + 128] = jnp.where(flip == 0, first, second).astype(bf16)
            dst[:, other : other + 128] = jnp.where(flip == 0, second, first).astype(bf16)


def heads_kernel(place_ref, heads_ref, out_ref):
    regroup(place_ref[0], place_ref[2], heads_ref, out_ref)


def order_heads(place, heads):
    return pl.pallas_call(
        heads_kernel,
        in_specs=[place_spec(), whole()],
        out_specs=whole(),
        out_shape=jax.ShapeDtypeStruct((128, 2048), bf16),
        name="order_heads",
    )(place, heads)


def weights_kernel(place_ref, own_ref, got_ref, first_ref, second_ref):
    high, flip = place_ref[0], place_ref[1]

    @pl.when(flip == place_ref[2])
    def _():
        regroup(high, flip, own_ref, first_ref)
        regroup(high, flip, got_ref, second_ref)

    @pl.when(flip != place_ref[2])
    def _():
        regroup(high, flip, got_ref, first_ref)
        regroup(high, flip, own_ref, second_ref)


def order_weights(place, own, got):
    return pl.pallas_call(
        weights_kernel,
        in_specs=[place_spec(), whole(), whole()],
        out_specs=[whole()] * 2,
        out_shape=[jax.ShapeDtypeStruct((288, 2048), bf16)] * 2,
        cost_estimate=pl.CostEstimate(flops=4000000, bytes_accessed=6000000, transcendentals=0),
        name="order_weights",
    )(place, own, got)


def pack(own_ref, got_ref, refs):
    total = jnp.zeros((288, 128), f32)
    for i in range(8):
        lane = slice(i * 128, i * 128 + 128)
        part = own_ref[:, lane] + got_ref[:, lane]
        total = total + part * part
        refs[i // 4][:, i % 4 * 128 : i % 4 * 128 + 128] = part.astype(bf16)
    return total


def first_kernel(own_ref, got_ref, a_ref, b_ref, sum_ref):
    sum_ref[...] = jnp.sum(pack(own_ref, got_ref, (a_ref, b_ref)), axis=0, keepdims=True)


def second_kernel(own_ref, got_ref, gown_ref, ggot_ref, first_ref, a_ref, b_ref, sum_ref):
    total = pack(own_ref, got_ref, (a_ref, b_ref))
    gain = gown_ref[...] + ggot_ref[...]
    total = jnp.sum(total) + jnp.sum(first_ref[...]) + jnp.sum(gain * gain)
    tile = jnp.concatenate([jnp.full((1, 128), total, f32), gain, jnp.zeros((4, 128), f32)], axis=0)
    for i in range(64):
        sum_ref[i] = tile


packed = jax.ShapeDtypeStruct((288, 512), bf16)
COST = pl.CostEstimate(flops=4000000, bytes_accessed=8000000, transcendentals=0)


def pack_first(own, got):
    return pl.pallas_call(
        first_kernel,
        in_specs=[whole()] * 2,
        out_specs=[whole()] * 3,
        out_shape=[packed, packed, jax.ShapeDtypeStruct((1, 128), f32)],
        cost_estimate=COST,
        name="pack_first_half",
    )(own, got)


def pack_second(own, got, gown, ggot, first):
    return pl.pallas_call(
        second_kernel,
        in_specs=[whole()] * 5,
        out_specs=[whole()] * 3,
        out_shape=[packed, packed, jax.ShapeDtypeStruct((64, 8, 128), f32)],
        cost_estimate=COST,
        name="pack_second_half",
    )(own, got, gown, ggot, first)


def combine_kernel(place_ref, sums_ref, a_ref, b_ref, c_ref, d_ref, out_ref):
    odd = lax.broadcasted_iota(jnp.int32, (32, 128), 0) % 2
    factors = []
    for h in range(2):
        rows = sums_ref[32 * h : 32 * h + 32, 0]
        for p in range(2):
            norm = jnp.sum(jnp.where(odd == p, rows, 0.0), axis=0, keepdims=True)
            factors.append(BOUND / jnp.maximum(jnp.sqrt(norm), BOUND))
    high_zero = place_ref[0] == 0
    core_zero = place_ref[2] == 0
    weights = []
    for d, c in SLOTS:
        pair = [jnp.where(high_zero, factors[2 * d + p], factors[2 - 2 * d + p]) for p in range(2)]
        weights.append(jnp.where(core_zero, pair[c], pair[1 - c]))
    refs = (a_ref, b_ref, c_ref, d_ref)

    def weighted(rows, lane):
        total = weights[0] * refs[0][rows, lane].astype(f32)
        for w, ref in zip(weights[1:], refs[1:]):
            total = total + w * ref[rows, lane].astype(f32)
        return total

    gain = jnp.zeros((3, 128), f32)
    for w, (d, c) in zip(weights, SLOTS):
        row = (place_ref[0] ^ d) * 32 + place_ref[1] * 16 + place_ref[3] * 2 + (place_ref[2] ^ c)
        gain = gain + w * sums_ref[row][1:4]
    high = gain.astype(bf16).astype(f32)
    extra = jnp.concatenate([high, gain - high, jnp.zeros((10, 128), f32)], axis=0).astype(bf16)
    left = lax.broadcasted_iota(jnp.int32, (144, 128), 1) < 64
    for j in range(4):
        part = weighted(slice(0, 288), slice(j * 128, j * 128 + 128))
        low, up = part[:144], part[144:]
        out_ref[2 * j, :144] = jnp.where(left, low, pltpu.roll(up, 64, 1)).astype(bf16)
        out_ref[2 * j + 1, :144] = jnp.where(left, pltpu.roll(low, 64, 1), up).astype(bf16)
        out_ref[2 * j, 144:] = extra
        out_ref[2 * j + 1, 144:] = extra


def combine(place, sums, parts):
    return pl.pallas_call(
        combine_kernel,
        in_specs=[place_spec()] + [whole()] * 5,
        out_specs=whole(),
        out_shape=jax.ShapeDtypeStruct((8, 160, 128), bf16),
        name="clip_and_combine",
    )(place, sums, *parts)


def finish_kernel(parts_ref, noise_ref, gain_noise_ref, out_ref, gain_ref):
    total = parts_ref[0].astype(f32)
    for i in range(1, 8):
        total = total + parts_ref[i].astype(f32)
    body = total[:144]
    rows = jnp.concatenate([body, pltpu.roll(body, 64, 1)], axis=0).T
    out_ref[...] = (rows[:64] + noise_ref[...]) * (1.0 / 32.0)
    gain_ref[...] = (total[144:147] + total[147:150] + gain_noise_ref[...]) * (1.0 / 32.0)


def finish(parts, noise, gain_noise):
    return pl.pallas_call(
        finish_kernel,
        out_shape=[jax.ShapeDtypeStruct((64, 288), f32), jax.ShapeDtypeStruct((3, 128), f32)],
        name="sum_and_noise",
    )(parts, noise, gain_noise)


def lanes(vector):
    return jnp.pad(vector, (0, 96)).reshape(3, 128)


def turn(x):
    return lax.ppermute(x, ("core", "xl"), [(0, 0), (1, 2), (2, 1), (3, 3)])


def to_owner(x, flip_high, flip_core):
    pairs = []
    for h in range(2):
        for c in range(2):
            for p in range(2):
                pairs.append((h * 4 + c * 2 + p, (h ^ flip_high) * 4 + (p ^ flip_core) * 2 + c))
    return lax.ppermute(x, ("xh", "core", "xl"), pairs)


def local(head_outputs, out_weight, norm_gain, cotangent, loss_mask, weight_noise, gain_noise):
    xl = lax.axis_index("xl")
    core = lax.axis_index("core")
    place = jnp.stack([lax.axis_index("xh"), xl, core, lax.axis_index("y")]).astype(jnp.int32)
    turned = turn(order_heads(place, head_outputs))
    heads = lax.all_gather(turned, "y", axis=0, tiled=True)
    masked = cotangent * loss_mask[:, None].astype(bf16)
    pieces = masked.reshape(128, 8, 2, 288).transpose(1, 2, 3, 0)
    low, high = pieces[:, 0], pieces[:, 1]
    ordered = jnp.concatenate(
        [jnp.where(xl == 0, low, high), jnp.where(xl == 0, high, low)], axis=1
    )
    arrived = turn(lax.all_to_all(ordered, "y", split_axis=0, concat_axis=0, tiled=True))
    weight_t, own_gain, _ = lax.optimization_barrier((out_weight.T, norm_gain, turned))
    weight_got, gain_got = swap(weight_t, "xl"), swap(own_gain, "xl")
    straight = xl == core
    weights = jnp.concatenate(order_weights(place, weight_t, weight_got), axis=0)
    gain = jnp.concatenate(
        [jnp.where(straight, own_gain, gain_got), jnp.where(straight, gain_got, own_gain)]
    )
    heads, weights, arrived, gain = lax.optimization_barrier((heads, weights, arrived, gain))
    gain = gain[:, None]
    other_heads = swap(heads, "core")
    arrived = arrived.transpose(1, 0, 2).reshape(576, 1024).astype(f32)
    projected = lax.dot_general(
        weights, heads, (((1,), (1,)), ((), ())), preferred_element_type=f32
    )
    stats = jnp.stack(
        [jnp.sum(projected * projected, axis=0), jnp.sum(projected * gain * arrived, axis=0)]
    )
    stats = jnp.sum(
        lax.all_to_all(
            jnp.broadcast_to(stats[None], (8, 2, 1024)), "y", split_axis=0, concat_axis=0, tiled=True
        ),
        axis=0,
    )
    inverse = lax.rsqrt(stats[0:1] / D + epsilon)
    products = stats[1:2]
    back_grad = (
        inverse * gain * arrived - projected * (inverse * inverse * inverse * products / D)
    ).astype(bf16)
    contract = (((1,), (0,)), ((), ()))
    own_grad, other_grad = back_grad[:288], back_grad[288:]
    got_grad = swap(other_grad, "core")

    def delta(grad, columns):
        return lax.dot_general(grad, columns, contract, preferred_element_type=f32)

    own_first, own_second = delta(own_grad, heads[:, :1024]), delta(own_grad, heads[:, 1024:])
    own_first, own_second, got_grad = lax.optimization_barrier((own_first, own_second, got_grad))
    gain_part = jnp.sum(arrived * projected * inverse, axis=1)
    gain_own, gain_got = lanes(gain_part[:288]), swap(lanes(gain_part[288:]), "core")
    a, b, first_sum = pack_first(own_first, delta(got_grad, other_heads[:, :1024]))
    c, d, squares = pack_second(own_second, delta(got_grad, other_heads[:, 1024:]), gain_own, gain_got, first_sum)
    a, b = to_owner(a, *SLOTS[0]), to_owner(b, *SLOTS[1])
    a, b, c, d = lax.optimization_barrier((a, b, c, d))
    parts = [a, b, to_owner(c, *SLOTS[2]), to_owner(d, *SLOTS[3])]
    sums = lax.all_to_all(squares, ("xh", "core", "y", "xl"), split_axis=0, concat_axis=0, tiled=True)
    chip = combine(place, sums, parts)
    over_z = lax.all_to_all(chip, "z", split_axis=0, concat_axis=0, tiled=True)
    update, gain_update = finish(over_z, weight_noise, lanes(gain_noise))
    return update, gain_update.reshape(384)[:288]


def solution(mesh):
    split_mesh = Mesh(mesh.devices.reshape(2, 8, 2, 8, 2), CLIENT + FSDP)
    both = CLIENT + FSDP
    placed = (
        P(both, None),
        P(None, FSDP),
        P(FSDP),
        P(both, None),
        P(both),
        P(CLIENT, FSDP),
        P(FSDP),
    )
    return jax.shard_map(
        local,
        mesh=split_mesh,
        in_specs=placed,
        out_specs=(P(CLIENT, FSDP), P(FSDP)),
        check_vma=False,
    )
```

```python
import functools
import math

import jax
import jax.numpy as jnp
from jax import lax
from jax.experimental import pallas as pl
from jax.experimental.pallas import tpu as pltpu
from jax.sharding import Mesh, PartitionSpec as P

D = 4608
HD = 2048
epsilon = 1e-06
CLIENT = ("xh", "z", "core")
FSDP = ("y", "xl")
BOUND = math.sqrt(HD * D)
f32 = jnp.float32
bf16 = jnp.bfloat16


def swap(x, axis):
    return lax.ppermute(x, axis, [(0, 1), (1, 0)])


def full(shape):
    return pl.BlockSpec(shape, lambda *i: (0,) * len(shape))


def place_spec():
    return pl.BlockSpec(memory_space=pltpu.SMEM)


def whole():
    return pl.BlockSpec(memory_space=pltpu.VMEM)


SLOTS = ((1, 0), (0, 1), (0, 0), (1, 1))


def grad_kernel(proj_ref, masked_ref, gain_ref, stats_ref, keep_ref, send_ref, gain_keep_ref):
    stats = stats_ref[0]
    for i in range(1, 8):
        stats = stats + stats_ref[i]
    inverse = lax.rsqrt(stats[0:1] / D + epsilon)
    coefficient = inverse * inverse * inverse * stats[1:2] / D
    gains = []
    for half, out in enumerate((keep_ref, send_ref)):
        rows = slice(288 * half, 288 * half + 288)
        gain = gain_ref[rows]
        total = jnp.zeros((288, 128), f32)
        for i in range(8):
            lane = slice(128 * i, 128 * i + 128)
            p = proj_ref[rows, lane]
            m = masked_ref[i, rows].astype(f32) * inverse[:, lane]
            out[:288, lane] = (gain * m - p * coefficient[:, lane]).astype(bf16)
            total += m * p
        row = jnp.sum(total.T, axis=0, keepdims=True)
        row = jnp.concatenate([row, jnp.zeros((1, 96), f32)], axis=1)
        gains.append(jnp.concatenate([row[:, 0:128], row[:, 128:256], row[:, 256:384]], axis=0))
    gain_keep_ref[...] = gains[0]
    high = gains[1].astype(bf16).astype(f32)
    extra = jnp.concatenate([high, gains[1] - high, jnp.zeros((10, 128), f32)], axis=0).astype(bf16)
    for i in range(8):
        send_ref[288:, 128 * i : 128 * i + 128] = extra


def gradients(projected, masked, gain, stats):
    return pl.pallas_call(
        grad_kernel,
        in_specs=[whole()] * 4,
        out_specs=[whole()] * 3,
        out_shape=[
            jax.ShapeDtypeStruct((288, 1024), bf16),
            jax.ShapeDtypeStruct((304, 1024), bf16),
            jax.ShapeDtypeStruct((3, 128), f32),
        ],
        cost_estimate=pl.CostEstimate(flops=4000000, bytes_accessed=6000000, transcendentals=0),
        name="gradients",
    )(projected, masked, gain, stats)


def delta_kernel(place_ref, keep_ref, got_ref, gain_ref, heads_ref, other_ref, *rest):
    outs, sum_ref, total = rest[:4], rest[4], rest[5]
    step = pl.program_id(0)
    value = jnp.dot(keep_ref[...], heads_ref[...], preferred_element_type=f32)
    value = value + jnp.dot(got_ref[:288], other_ref[...], preferred_element_type=f32)
    squares = value * value
    folded = squares[:, :128] + squares[:, 128:256] + squares[:, 256:384] + squares[:, 384:]
    left = lax.broadcasted_iota(jnp.int32, (288, 128), 1) < 64
    zero = place_ref[1] == 0
    pieces = []
    for j in range(2):
        a, b = value[:, 256 * j : 256 * j + 128], value[:, 256 * j + 128 : 256 * j + 256]
        first = jnp.where(left, a, pltpu.roll(b, 64, 1))
        second = jnp.where(left, pltpu.roll(a, 64, 1), b)
        pieces.append((jnp.where(zero, first, second).astype(bf16), jnp.where(zero, second, first).astype(bf16)))

    @pl.when(step == 0)
    def _():
        total[...] = folded

    @pl.when(step > 0)
    def _():
        total[...] += folded

    for n in range(4):

        @pl.when(step == n)
        def _():
            d = 1 - n // 2
            for j in range(2):
                lane = slice((n % 2) * 256 + j * 128, (n % 2) * 256 + j * 128 + 128)
                for c in range(2):
                    outs[SLOTS.index((d, c))][:, lane] = pieces[j][c]

    @pl.when(step == 3)
    def _():
        extra = got_ref[288:, :128].astype(f32)
        gain = gain_ref[...] + extra[0:3] + extra[3:6]
        norm = jnp.sum(total[...]) + jnp.sum(gain * gain)
        tile = jnp.concatenate([jnp.full((1, 128), norm, f32), gain, jnp.zeros((4, 128), f32)], axis=0)
        for i in range(64):
            sum_ref[i] = tile


def deltas(place, keep, got, gain, heads, other_heads):
    fixed = lambda shape: pl.BlockSpec(shape, lambda n, place: (0,) * len(shape))
    columns = pl.BlockSpec((1024, 512), lambda n, place: (0, (place[0] ^ (1 - n // 2)) * 2 + n % 2))
    packed = jax.ShapeDtypeStruct((288, 512), bf16)
    return pl.pallas_call(
        delta_kernel,
        grid_spec=pltpu.PrefetchScalarGridSpec(
            num_scalar_prefetch=1,
            grid=(4,),
            in_specs=[whole(), whole(), whole(), columns, columns],
            out_specs=[fixed((288, 512))] * 4 + [fixed((64, 8, 128))],
            scratch_shapes=[pltpu.VMEM((288, 128), f32)],
        ),
        out_shape=[packed] * 4 + [jax.ShapeDtypeStruct((64, 8, 128), f32)],
        cost_estimate=pl.CostEstimate(flops=4 * 288 * 1024 * 2048, bytes_accessed=12000000, transcendentals=0),
        name="deltas",
    )(place, keep, got, gain, heads, other_heads)


def combine_kernel(place_ref, sums_ref, a_ref, b_ref, c_ref, d_ref, out_ref):
    odd = lax.broadcasted_iota(jnp.int32, (32, 128), 0) % 2
    factors = []
    for h in range(2):
        rows = sums_ref[32 * h : 32 * h + 32, 0]
        for p in range(2):
            norm = jnp.sum(jnp.where(odd == p, rows, 0.0), axis=0, keepdims=True)
            factors.append(BOUND / jnp.maximum(jnp.sqrt(norm), BOUND))
    high_zero = place_ref[0] == 0
    core_zero = place_ref[2] == 0
    weights = []
    for d, c in SLOTS:
        pair = [jnp.where(high_zero, factors[2 * d + p], factors[2 - 2 * d + p]) for p in range(2)]
        weights.append(jnp.where(core_zero, pair[c], pair[1 - c]))
    refs = (a_ref, b_ref, c_ref, d_ref)

    def weighted(rows, lane):
        total = weights[0] * refs[0][rows, lane].astype(f32)
        for w, ref in zip(weights[1:], refs[1:]):
            total = total + w * ref[rows, lane].astype(f32)
        return total

    gain = jnp.zeros((3, 128), f32)
    for w, (d, c) in zip(weights, SLOTS):
        row = (place_ref[0] ^ d) * 32 + place_ref[1] * 16 + place_ref[3] * 2 + (place_ref[2] ^ c)
        gain = gain + w * sums_ref[row][1:4]
    high = gain.astype(bf16).astype(f32)
    extra = jnp.concatenate([high, gain - high, jnp.zeros((10, 128), f32)], axis=0).astype(bf16)
    left = lax.broadcasted_iota(jnp.int32, (144, 128), 1) < 64
    for j in range(4):
        part = weighted(slice(0, 288), slice(j * 128, j * 128 + 128))
        low, up = part[:144], part[144:]
        out_ref[2 * j, :144] = jnp.where(left, low, pltpu.roll(up, 64, 1)).astype(bf16)
        out_ref[2 * j + 1, :144] = jnp.where(left, pltpu.roll(low, 64, 1), up).astype(bf16)
        out_ref[2 * j, 144:] = extra
        out_ref[2 * j + 1, 144:] = extra


def combine(place, sums, parts):
    return pl.pallas_call(
        combine_kernel,
        in_specs=[place_spec()] + [whole()] * 5,
        out_specs=whole(),
        out_shape=jax.ShapeDtypeStruct((8, 160, 128), bf16),
        name="clip_and_combine",
    )(place, sums, *parts)


def finish_kernel(parts_ref, noise_ref, gain_noise_ref, out_ref, gain_ref):
    total = parts_ref[0].astype(f32)
    for i in range(1, 8):
        total = total + parts_ref[i].astype(f32)
    body = total[:144]
    rows = jnp.concatenate([body, pltpu.roll(body, 64, 1)], axis=0).T
    out_ref[...] = (rows[:64] + noise_ref[...]) * (1.0 / 32.0)
    gain_ref[...] = (total[144:147] + total[147:150] + gain_noise_ref[...]) * (1.0 / 32.0)


def finish(parts, noise, gain_noise):
    return pl.pallas_call(
        finish_kernel,
        out_shape=[jax.ShapeDtypeStruct((64, 288), f32), jax.ShapeDtypeStruct((3, 128), f32)],
        name="sum_and_noise",
    )(parts, noise, gain_noise)


def lanes(vector):
    return jnp.pad(vector, (0, 96)).reshape(3, 128)


def turn(x):
    return lax.ppermute(x, ("core", "xl"), [(0, 0), (1, 2), (2, 1), (3, 3)])


def to_owner(x, flip_high, flip_core):
    pairs = []
    for h in range(2):
        for c in range(2):
            for p in range(2):
                pairs.append((h * 4 + c * 2 + p, (h ^ flip_high) * 4 + (p ^ flip_core) * 2 + c))
    return lax.ppermute(x, ("xh", "core", "xl"), pairs)


def local(head_outputs, out_weight, norm_gain, cotangent, loss_mask, weight_noise, gain_noise):
    xl = lax.axis_index("xl")
    core = lax.axis_index("core")
    place = jnp.stack([lax.axis_index("xh"), xl, core, lax.axis_index("y")]).astype(jnp.int32)
    turned = turn(head_outputs)
    heads = lax.all_gather(turned, "y", axis=0, tiled=True)
    masked = cotangent * loss_mask[:, None].astype(bf16)
    pieces = masked.reshape(128, 8, 2, 288).transpose(1, 2, 3, 0)
    low, high = pieces[:, 0], pieces[:, 1]
    ordered = jnp.concatenate(
        [jnp.where(xl == 0, low, high), jnp.where(xl == 0, high, low)], axis=1
    )
    arrived = turn(lax.all_to_all(ordered, "y", split_axis=0, concat_axis=0, tiled=True))
    weight_t, own_gain, _ = lax.optimization_barrier((out_weight.T, norm_gain, turned))
    weight_got, gain_got = swap(weight_t, "xl"), swap(own_gain, "xl")
    straight = xl == core
    weights = jnp.concatenate(
        [jnp.where(straight, weight_t, weight_got), jnp.where(straight, weight_got, weight_t)], axis=0
    )
    gain = jnp.concatenate(
        [jnp.where(straight, own_gain, gain_got), jnp.where(straight, gain_got, own_gain)]
    )
    heads, weights, arrived, gain = lax.optimization_barrier((heads, weights, arrived, gain))
    gain = gain[:, None]
    other_heads = swap(heads, "core")
    cotangents = arrived.transpose(1, 0, 2).reshape(576, 1024).astype(f32)
    projected = lax.dot_general(
        weights, heads, (((1,), (1,)), ((), ())), preferred_element_type=f32
    )
    stats = jnp.stack(
        [jnp.sum(projected * projected, axis=0), jnp.sum(projected * gain * cotangents, axis=0)]
    )
    stats = lax.all_to_all(
        jnp.broadcast_to(stats[None], (8, 2, 1024)), "y", split_axis=0, concat_axis=0, tiled=True
    )
    keep_grad, send_grad, gain_keep = gradients(projected, arrived, gain, stats)
    *packed, squares = deltas(place, keep_grad, swap(send_grad, "core"), gain_keep, heads, other_heads)
    parts = [to_owner(x, *slot) for x, slot in zip(packed, SLOTS)]
    sums = lax.all_to_all(squares, ("xh", "core", "y", "xl"), split_axis=0, concat_axis=0, tiled=True)
    chip = combine(place, sums, parts)
    over_z = lax.all_to_all(chip, "z", split_axis=0, concat_axis=0, tiled=True)
    update, gain_update = finish(over_z, weight_noise, lanes(gain_noise))
    return update, gain_update.reshape(384)[:288]


def solution(mesh):
    split_mesh = Mesh(mesh.devices.reshape(2, 8, 2, 8, 2), CLIENT + FSDP)
    both = CLIENT + FSDP
    placed = (
        P(both, None),
        P(None, FSDP),
        P(FSDP),
        P(both, None),
        P(both),
        P(CLIENT, FSDP),
        P(FSDP),
    )
    return jax.shard_map(
        local,
        mesh=split_mesh,
        in_specs=placed,
        out_specs=(P(CLIENT, FSDP), P(FSDP)),
        check_vma=False,
    )
```

```python
import functools
import math

import jax
import jax.numpy as jnp
from jax import lax
from jax.experimental import pallas as pl
from jax.experimental.pallas import tpu as pltpu
from jax.sharding import Mesh, PartitionSpec as P

D = 4608
HD = 2048
epsilon = 1e-06
CLIENT = ("xh", "z", "core")
FSDP = ("y", "xl")
BOUND = math.sqrt(HD * D)
f32 = jnp.float32
bf16 = jnp.bfloat16


def swap(x, axis):
    return lax.ppermute(x, axis, [(0, 1), (1, 0)])


def full(shape):
    return pl.BlockSpec(shape, lambda *i: (0,) * len(shape))


def place_spec():
    return pl.BlockSpec(memory_space=pltpu.SMEM)


def whole():
    return pl.BlockSpec(memory_space=pltpu.VMEM)


BLOCKS = (0, -1, 1, -2, 2, -3, 3, 4)


SLOTS = ((1, 0), (0, 1), (0, 0), (1, 1))


def block_lanes(place_ref, i):
    source = (place_ref[3] + BLOCKS[i] + 8) & 7
    return pl.ds(pl.multiple_of(source * 128, 128), 128), source


def block_of(refs, rows, i):
    ref, i = (refs[0], i) if i < 5 else (refs[1], i - 5) if i < 7 else (refs[2], 0)
    return ref[rows, 128 * i : 128 * i + 128]


def sums_kernel(place_ref, *rest):
    refs, (masked_ref, gain_ref, out_ref, row) = rest[:3], rest[3:]
    for i in range(8):
        lane, source = block_lanes(place_ref, i)
        squares = jnp.zeros((1, 128), f32)
        products = jnp.zeros((1, 128), f32)
        for half in range(2):
            rows = slice(288 * half, 288 * half + 288)
            p = block_of(refs, rows, i)
            squares += jnp.sum(p * p, axis=0, keepdims=True)
            products += jnp.sum(p * gain_ref[rows] * masked_ref[source, rows].astype(f32), axis=0, keepdims=True)
        row[0:1, lane] = squares
        row[1:2, lane] = products
    for i in range(8):
        out_ref[i] = row[...]


def token_sums(place, projected, masked, gain):
    return pl.pallas_call(
        sums_kernel,
        in_specs=[place_spec()] + [whole()] * 5,
        out_specs=whole(),
        out_shape=jax.ShapeDtypeStruct((8, 2, 1024), f32),
        scratch_shapes=[pltpu.VMEM((2, 1024), f32)],
        cost_estimate=pl.CostEstimate(flops=4000000, bytes_accessed=5000000, transcendentals=0),
        name="token_sums",
    )(place, *projected, masked, gain)


def grad_kernel(place_ref, *rest):
    refs, (masked_ref, gain_ref, stats_ref, keep_ref, send_ref, gain_keep_ref, row) = rest[:3], rest[3:]
    stats = stats_ref[0]
    for i in range(1, 8):
        stats = stats + stats_ref[i]
    inverse = lax.rsqrt(stats[0:1] / D + epsilon)
    row[0:1] = inverse
    row[1:2] = inverse * inverse * inverse * stats[1:2] / D
    gains = []
    for half, out in enumerate((keep_ref, send_ref)):
        rows = slice(288 * half, 288 * half + 288)
        gain = gain_ref[rows]
        total = jnp.zeros((288, 128), f32)
        for i in range(8):
            lane, source = block_lanes(place_ref, i)
            p = block_of(refs, rows, i)
            m = masked_ref[source, rows].astype(f32) * row[0:1, lane]
            out[:288, 128 * i : 128 * i + 128] = (gain * m - p * row[1:2, lane]).astype(bf16)
            total += m * p
        line = jnp.sum(total.T, axis=0, keepdims=True)
        line = jnp.concatenate([line, jnp.zeros((1, 96), f32)], axis=1)
        gains.append(jnp.concatenate([line[:, 0:128], line[:, 128:256], line[:, 256:384]], axis=0))
    gain_keep_ref[...] = gains[0]
    high = gains[1].astype(bf16).astype(f32)
    extra = jnp.concatenate([high, gains[1] - high, jnp.zeros((10, 128), f32)], axis=0).astype(bf16)
    for i in range(8):
        send_ref[288:, 128 * i : 128 * i + 128] = extra


def gradients(place, projected, masked, gain, stats):
    return pl.pallas_call(
        grad_kernel,
        in_specs=[place_spec()] + [whole()] * 6,
        out_specs=[whole()] * 3,
        out_shape=[
            jax.ShapeDtypeStruct((288, 1024), bf16),
            jax.ShapeDtypeStruct((304, 1024), bf16),
            jax.ShapeDtypeStruct((3, 128), f32),
        ],
        scratch_shapes=[pltpu.VMEM((2, 1024), f32)],
        cost_estimate=pl.CostEstimate(flops=4000000, bytes_accessed=6000000, transcendentals=0),
        name="gradients",
    )(place, *projected, masked, gain, stats)


def delta_kernel(place_ref, keep_ref, got_ref, gain_ref, *rest):
    heads, others, outs, (sum_ref, total) = rest[:3], rest[3:6], rest[6:10], rest[10:]
    step = pl.program_id(0)
    value = jnp.zeros((288, 512), f32)
    for grads, refs in ((keep_ref, heads), (got_ref, others)):
        start = 0
        for ref in refs:
            grad = grads[:288, start : start + ref.shape[0]]
            value = value + jnp.dot(grad, ref[...], preferred_element_type=f32)
            start += ref.shape[0]
    squares = value * value
    folded = squares[:, :128] + squares[:, 128:256] + squares[:, 256:384] + squares[:, 384:]
    left = lax.broadcasted_iota(jnp.int32, (288, 128), 1) < 64
    zero = place_ref[1] == 0
    pieces = []
    for j in range(2):
        a, b = value[:, 256 * j : 256 * j + 128], value[:, 256 * j + 128 : 256 * j + 256]
        first = jnp.where(left, a, pltpu.roll(b, 64, 1))
        second = jnp.where(left, pltpu.roll(a, 64, 1), b)
        pieces.append((jnp.where(zero, first, second).astype(bf16), jnp.where(zero, second, first).astype(bf16)))

    @pl.when(step == 0)
    def _():
        total[...] = folded

    @pl.when(step > 0)
    def _():
        total[...] += folded

    for n in range(4):

        @pl.when(step == n)
        def _():
            d = 1 - n // 2
            for j in range(2):
                lane = slice((n % 2) * 256 + j * 128, (n % 2) * 256 + j * 128 + 128)
                for c in range(2):
                    outs[SLOTS.index((d, c))][:, lane] = pieces[j][c]

    @pl.when(step == 3)
    def _():
        extra = got_ref[288:, :128].astype(f32)
        gain = gain_ref[...] + extra[0:3] + extra[3:6]
        norm = jnp.sum(total[...]) + jnp.sum(gain * gain)
        tile = jnp.concatenate([jnp.full((1, 128), norm, f32), gain, jnp.zeros((4, 128), f32)], axis=0)
        for i in range(64):
            sum_ref[i] = tile


def deltas(place, keep, got, gain, *heads):
    fixed = lambda shape: pl.BlockSpec(shape, lambda n, place: (0,) * len(shape))
    index = lambda n, place: (0, (place[0] ^ (1 - n // 2)) * 2 + n % 2)
    columns = [pl.BlockSpec((size, 512), index) for size in (640, 256, 128)]
    packed = jax.ShapeDtypeStruct((288, 512), bf16)
    return pl.pallas_call(
        delta_kernel,
        grid_spec=pltpu.PrefetchScalarGridSpec(
            num_scalar_prefetch=1,
            grid=(4,),
            in_specs=[whole(), whole(), whole()] + columns * 2,
            out_specs=[fixed((288, 512))] * 4 + [fixed((64, 8, 128))],
            scratch_shapes=[pltpu.VMEM((288, 128), f32)],
        ),
        out_shape=[packed] * 4 + [jax.ShapeDtypeStruct((64, 8, 128), f32)],
        cost_estimate=pl.CostEstimate(flops=4 * 288 * 1024 * 2048, bytes_accessed=12000000, transcendentals=0),
        name="deltas",
    )(place, keep, got, gain, *heads)


def combine_kernel(place_ref, sums_ref, a_ref, b_ref, c_ref, d_ref, out_ref):
    odd = lax.broadcasted_iota(jnp.int32, (32, 128), 0) % 2
    factors = []
    for h in range(2):
        rows = sums_ref[32 * h : 32 * h + 32, 0]
        for p in range(2):
            norm = jnp.sum(jnp.where(odd == p, rows, 0.0), axis=0, keepdims=True)
            factors.append(BOUND / jnp.maximum(jnp.sqrt(norm), BOUND))
    high_zero = place_ref[0] == 0
    core_zero = place_ref[2] == 0
    weights = []
    for d, c in SLOTS:
        pair = [jnp.where(high_zero, factors[2 * d + p], factors[2 - 2 * d + p]) for p in range(2)]
        weights.append(jnp.where(core_zero, pair[c], pair[1 - c]))
    refs = (a_ref, b_ref, c_ref, d_ref)

    def weighted(rows, lane):
        total = weights[0] * refs[0][rows, lane].astype(f32)
        for w, ref in zip(weights[1:], refs[1:]):
            total = total + w * ref[rows, lane].astype(f32)
        return total

    gain = jnp.zeros((3, 128), f32)
    for w, (d, c) in zip(weights, SLOTS):
        row = (place_ref[0] ^ d) * 32 + place_ref[1] * 16 + place_ref[3] * 2 + (place_ref[2] ^ c)
        gain = gain + w * sums_ref[row][1:4]
    high = gain.astype(bf16).astype(f32)
    extra = jnp.concatenate([high, gain - high, jnp.zeros((10, 128), f32)], axis=0).astype(bf16)
    left = lax.broadcasted_iota(jnp.int32, (144, 128), 1) < 64
    for j in range(4):
        part = weighted(slice(0, 288), slice(j * 128, j * 128 + 128))
        low, up = part[:144], part[144:]
        out_ref[2 * j, :144] = jnp.where(left, low, pltpu.roll(up, 64, 1)).astype(bf16)
        out_ref[2 * j + 1, :144] = jnp.where(left, pltpu.roll(low, 64, 1), up).astype(bf16)
        out_ref[2 * j, 144:] = extra
        out_ref[2 * j + 1, 144:] = extra


def combine(place, sums, parts):
    return pl.pallas_call(
        combine_kernel,
        in_specs=[place_spec()] + [whole()] * 5,
        out_specs=whole(),
        out_shape=jax.ShapeDtypeStruct((8, 160, 128), bf16),
        name="clip_and_combine",
    )(place, sums, *parts)


def finish_kernel(parts_ref, noise_ref, gain_noise_ref, out_ref, gain_ref):
    total = parts_ref[0].astype(f32)
    for i in range(1, 8):
        total = total + parts_ref[i].astype(f32)
    body = total[:144]
    rows = jnp.concatenate([body, pltpu.roll(body, 64, 1)], axis=0).T
    out_ref[...] = (rows[:64] + noise_ref[...]) * (1.0 / 32.0)
    gain_ref[...] = (total[144:147] + total[147:150] + gain_noise_ref[...]) * (1.0 / 32.0)


def finish(parts, noise, gain_noise):
    return pl.pallas_call(
        finish_kernel,
        out_shape=[jax.ShapeDtypeStruct((64, 288), f32), jax.ShapeDtypeStruct((3, 128), f32)],
        name="sum_and_noise",
    )(parts, noise, gain_noise)


def lanes(vector):
    return jnp.pad(vector, (0, 96)).reshape(3, 128)


def turn(x):
    return lax.ppermute(x, ("core", "xl"), [(0, 0), (1, 2), (2, 1), (3, 3)])


def along_y(x, step):
    return lax.ppermute(x, "y", [(i, (i + step) % 8) for i in range(8)])


def to_owner(x, flip_high, flip_core):
    pairs = []
    for h in range(2):
        for c in range(2):
            for p in range(2):
                pairs.append((h * 4 + c * 2 + p, (h ^ flip_high) * 4 + (p ^ flip_core) * 2 + c))
    return lax.ppermute(x, ("xh", "core", "xl"), pairs)


def local(head_outputs, out_weight, norm_gain, cotangent, loss_mask, weight_noise, gain_noise):
    xl = lax.axis_index("xl")
    core = lax.axis_index("core")
    place = jnp.stack([lax.axis_index("xh"), xl, core, lax.axis_index("y")]).astype(jnp.int32)
    masked = cotangent * loss_mask[:, None].astype(bf16)
    pieces = masked.reshape(128, 8, 2, 288).transpose(1, 2, 3, 0)
    low, high = pieces[:, 0], pieces[:, 1]
    ordered = jnp.concatenate(
        [jnp.where(xl == 0, low, high), jnp.where(xl == 0, high, low)], axis=1
    )
    ordered, turned = lax.optimization_barrier((ordered, turn(head_outputs)))
    arrived = lax.all_to_all(ordered, "y", split_axis=0, concat_axis=0, tiled=True)
    weight_t, own_gain, _ = lax.optimization_barrier((out_weight.T, norm_gain, turned))
    weight_got, gain_got = swap(weight_t, "xl"), swap(own_gain, "xl")
    straight = xl == core
    weights = jnp.concatenate(
        [jnp.where(straight, weight_t, weight_got), jnp.where(straight, weight_got, weight_t)], axis=0
    )
    gain = jnp.concatenate(
        [jnp.where(straight, own_gain, gain_got), jnp.where(straight, gain_got, own_gain)]
    )[:, None]

    def project(heads):
        return lax.dot_general(weights, heads, (((1,), (1,)), ((), ())), preferred_element_type=f32)

    up, down = [turned], [turned]
    for _ in range(2):
        up.append(along_y(up[-1], 1))
        down.append(along_y(down[-1], -1))
    arrived, weights, gain, up[2], down[2] = lax.optimization_barrier((arrived, weights, gain, up[2], down[2]))
    arrived = turn(arrived)
    up.append(along_y(up[2], 1))
    down.append(along_y(down[2], -1))
    heads = [jnp.concatenate([turned, up[1], down[1], up[2], down[2]], axis=0)]
    projected = [project(heads[0])]
    others = [swap(heads[0], "core")]
    projected[0], up[3], down[3] = lax.optimization_barrier((projected[0], up[3], down[3]))
    low, high = along_y(up[3][:64], 1), along_y(down[3][64:], -1)
    heads.append(jnp.concatenate([up[3], down[3]], axis=0))
    projected.append(project(heads[1]))
    others.append(swap(heads[1], "core"))
    projected[1], low, high = lax.optimization_barrier((projected[1], low, high))
    heads.append(jnp.concatenate([low, high], axis=0))
    projected.append(project(heads[2]))
    others.append(swap(heads[2], "core"))
    stats = token_sums(place, projected, arrived, gain)
    stats = lax.all_to_all(stats, "y", split_axis=0, concat_axis=0, tiled=True)
    keep_grad, send_grad, gain_keep = gradients(place, projected, arrived, gain, stats)
    got_grad = swap(send_grad, "core")
    *packed, squares = deltas(place, keep_grad, got_grad, gain_keep, *heads, *others)
    parts = [to_owner(x, *slot) for x, slot in zip(packed, SLOTS)]
    sums = lax.all_to_all(squares, ("xh", "core", "y", "xl"), split_axis=0, concat_axis=0, tiled=True)
    chip = combine(place, sums, parts)
    over_z = lax.all_to_all(chip, "z", split_axis=0, concat_axis=0, tiled=True)
    update, gain_update = finish(over_z, weight_noise, lanes(gain_noise))
    return update, gain_update.reshape(384)[:288]


def solution(mesh):
    split_mesh = Mesh(mesh.devices.reshape(2, 8, 2, 8, 2), CLIENT + FSDP)
    both = CLIENT + FSDP
    placed = (
        P(both, None),
        P(None, FSDP),
        P(FSDP),
        P(both, None),
        P(both),
        P(CLIENT, FSDP),
        P(FSDP),
    )
    return jax.shard_map(
        local,
        mesh=split_mesh,
        in_specs=placed,
        out_specs=(P(CLIENT, FSDP), P(FSDP)),
        check_vma=False,
    )
```

```python
import functools
import math

import jax
import jax.numpy as jnp
from jax import lax
from jax.experimental import pallas as pl
from jax.experimental.pallas import tpu as pltpu
from jax.sharding import Mesh, PartitionSpec as P

D = 4608
HD = 2048
epsilon = 1e-06
CLIENT = ("xh", "z", "core")
FSDP = ("y", "xl")
BOUND = math.sqrt(HD * D)
f32 = jnp.float32
bf16 = jnp.bfloat16


def swap(x, axis):
    return lax.ppermute(x, axis, [(0, 1), (1, 0)])


def full(shape):
    return pl.BlockSpec(shape, lambda *i: (0,) * len(shape))


def place_spec():
    return pl.BlockSpec(memory_space=pltpu.SMEM)


def whole():
    return pl.BlockSpec(memory_space=pltpu.VMEM)


BLOCKS = (0, -1, 1, -2, 2, -3, 3, 4)
SIZES = (384, 256, 256, 128)


SLOTS = ((1, 0), (0, 1), (0, 0), (1, 1))


def block_lanes(place_ref, i):
    source = (place_ref[3] + BLOCKS[i] + 8) & 7
    return pl.ds(pl.multiple_of(source * 128, 128), 128), source


def block_of(refs, rows, i):
    start = 128 * i
    for ref, size in zip(refs, SIZES):
        if start < size:
            return ref[rows, start : start + 128]
        start -= size


def project_block(place_ref, own_ref, got_ref, heads, out_ref, lane):
    own = (place_ref[1] ^ place_ref[2]) * 288
    contract = (((1,), (1,)), ((), ()))
    for start, ref in ((own, own_ref), (288 - own, got_ref)):
        value = lax.dot_general(ref[...], heads, contract, preferred_element_type=f32)
        out_ref[pl.ds(pl.multiple_of(start, 8), 288), lane] = value


def project_kernel(place_ref, own_ref, got_ref, *rest):
    blocks, (out_ref, heads_ref) = rest[:-2], rest[-2:]
    heads = jnp.concatenate([ref[...] for ref in blocks], axis=0)
    heads_ref[...] = heads
    project_block(place_ref, own_ref, got_ref, heads, out_ref, slice(None))


def project(place, own, got, *blocks):
    tokens = sum(x.shape[0] for x in blocks)
    return pl.pallas_call(
        project_kernel,
        in_specs=[place_spec()] + [whole()] * (2 + len(blocks)),
        out_specs=[whole()] * 2,
        out_shape=[jax.ShapeDtypeStruct((576, tokens), f32), jax.ShapeDtypeStruct((tokens, 2048), bf16)],
        cost_estimate=pl.CostEstimate(flops=1000, bytes_accessed=1000, transcendentals=0),
        name="project",
    )(place, own, got, *blocks)


def block_sums(place_ref, value, masked_ref, gain_ref, row, i):
    lane, source = block_lanes(place_ref, i)
    squares = jnp.zeros((1, 128), f32)
    products = jnp.zeros((1, 128), f32)
    for half in range(2):
        rows = slice(288 * half, 288 * half + 288)
        p = value(rows)
        squares += jnp.sum(p * p, axis=0, keepdims=True)
        products += jnp.sum(p * gain_ref[rows] * masked_ref[source, rows].astype(f32), axis=0, keepdims=True)
    row[0:1, lane] = squares
    row[1:2, lane] = products


def sums_kernel(place_ref, *rest):
    refs, (masked_ref, gain_ref, row) = rest[:3], rest[3:]
    row[...] = jnp.zeros((2, 1024), f32)
    for i in range(7):
        block_sums(place_ref, lambda rows, i=i: block_of(refs, rows, i), masked_ref, gain_ref, row, i)


def token_sums(place, projected, masked, gain):
    return pl.pallas_call(
        sums_kernel,
        in_specs=[place_spec()] + [whole()] * 5,
        out_specs=whole(),
        out_shape=jax.ShapeDtypeStruct((2, 1024), f32),
        cost_estimate=pl.CostEstimate(flops=1000, bytes_accessed=1000, transcendentals=0),
        name="token_sums",
    )(place, *projected, masked, gain)


def last_kernel(place_ref, own_ref, got_ref, low_ref, high_ref, masked_ref, gain_ref, sums_ref, out_ref, heads_ref, stats_ref, row):
    heads = jnp.concatenate([low_ref[...], high_ref[...]], axis=0)
    heads_ref[...] = heads
    project_block(place_ref, own_ref, got_ref, heads, out_ref, slice(None))
    row[...] = sums_ref[...]
    block_sums(place_ref, lambda rows: out_ref[rows], masked_ref, gain_ref, row, 7)
    for i in range(8):
        stats_ref[i] = row[...]


def project_last(place, own, got, low, high, masked, gain, sums):
    return pl.pallas_call(
        last_kernel,
        in_specs=[place_spec()] + [whole()] * 7,
        out_specs=[whole()] * 3,
        out_shape=[
            jax.ShapeDtypeStruct((576, 128), f32),
            jax.ShapeDtypeStruct((128, 2048), bf16),
            jax.ShapeDtypeStruct((8, 2, 1024), f32),
        ],
        scratch_shapes=[pltpu.VMEM((2, 1024), f32)],
        cost_estimate=pl.CostEstimate(flops=2 * 576 * 2048 * 128, bytes_accessed=6000000, transcendentals=0),
        name="project_last",
    )(place, own, got, low, high, masked, gain, sums)


def grad_kernel(place_ref, *rest):
    refs, (masked_ref, gain_ref, stats_ref, keep_ref, send_ref, gain_keep_ref, row) = rest[:4], rest[4:]
    stats = stats_ref[0]
    for i in range(1, 8):
        stats = stats + stats_ref[i]
    inverse = lax.rsqrt(stats[0:1] / D + epsilon)
    row[0:1] = inverse
    row[1:2] = inverse * inverse * inverse * stats[1:2] / D
    gains = []
    for half, out in enumerate((keep_ref, send_ref)):
        rows = slice(288 * half, 288 * half + 288)
        gain = gain_ref[rows]
        total = jnp.zeros((288, 128), f32)
        for i in range(8):
            lane, source = block_lanes(place_ref, i)
            p = block_of(refs, rows, i)
            m = masked_ref[source, rows].astype(f32) * row[0:1, lane]
            out[:288, 128 * i : 128 * i + 128] = (gain * m - p * row[1:2, lane]).astype(bf16)
            total += m * p
        line = jnp.sum(total.T, axis=0, keepdims=True)
        line = jnp.concatenate([line, jnp.zeros((1, 96), f32)], axis=1)
        gains.append(jnp.concatenate([line[:, 0:128], line[:, 128:256], line[:, 256:384]], axis=0))
    gain_keep_ref[...] = gains[0]
    high = gains[1].astype(bf16).astype(f32)
    extra = jnp.concatenate([high, gains[1] - high, jnp.zeros((10, 128), f32)], axis=0).astype(bf16)
    for i in range(8):
        send_ref[288:, 128 * i : 128 * i + 128] = extra


def gradients(place, projected, masked, gain, stats):
    return pl.pallas_call(
        grad_kernel,
        in_specs=[place_spec()] + [whole()] * 7,
        out_specs=[whole()] * 3,
        out_shape=[
            jax.ShapeDtypeStruct((288, 1024), bf16),
            jax.ShapeDtypeStruct((304, 1024), bf16),
            jax.ShapeDtypeStruct((3, 128), f32),
        ],
        scratch_shapes=[pltpu.VMEM((2, 1024), f32)],
        cost_estimate=pl.CostEstimate(flops=4000000, bytes_accessed=6000000, transcendentals=0),
        name="gradients",
    )(place, *projected, masked, gain, stats)


def delta_kernel(place_ref, keep_ref, got_ref, gain_ref, *rest):
    heads, others, outs, (sum_ref, total) = rest[:4], rest[4:8], rest[8:12], rest[12:]
    step = pl.program_id(0)
    value = jnp.zeros((288, 512), f32)
    for grads, refs in ((keep_ref, heads), (got_ref, others)):
        start = 0
        for ref in refs:
            grad = grads[:288, start : start + ref.shape[0]]
            value = value + jnp.dot(grad, ref[...], preferred_element_type=f32)
            start += ref.shape[0]
    squares = value * value
    folded = squares[:, :128] + squares[:, 128:256] + squares[:, 256:384] + squares[:, 384:]
    left = lax.broadcasted_iota(jnp.int32, (288, 128), 1) < 64
    zero = place_ref[1] == 0
    pieces = []
    for j in range(2):
        a, b = value[:, 256 * j : 256 * j + 128], value[:, 256 * j + 128 : 256 * j + 256]
        first = jnp.where(left, a, pltpu.roll(b, 64, 1))
        second = jnp.where(left, pltpu.roll(a, 64, 1), b)
        pieces.append((jnp.where(zero, first, second).astype(bf16), jnp.where(zero, second, first).astype(bf16)))

    @pl.when(step == 0)
    def _():
        total[...] = folded

    @pl.when(step > 0)
    def _():
        total[...] += folded

    for n in range(4):

        @pl.when(step == n)
        def _():
            d = 1 - n // 2
            for j in range(2):
                lane = slice((n % 2) * 256 + j * 128, (n % 2) * 256 + j * 128 + 128)
                for c in range(2):
                    outs[SLOTS.index((d, c))][:, lane] = pieces[j][c]

    @pl.when(step == 3)
    def _():
        extra = got_ref[288:, :128].astype(f32)
        gain = gain_ref[...] + extra[0:3] + extra[3:6]
        norm = jnp.sum(total[...]) + jnp.sum(gain * gain)
        tile = jnp.concatenate([jnp.full((1, 128), norm, f32), gain, jnp.zeros((4, 128), f32)], axis=0)
        for i in range(64):
            sum_ref[i] = tile


def deltas(place, keep, got, gain, *heads):
    fixed = lambda shape: pl.BlockSpec(shape, lambda n, place: (0,) * len(shape))
    index = lambda n, place: (0, (place[0] ^ (1 - n // 2)) * 2 + n % 2)
    columns = [pl.BlockSpec((size, 512), index) for size in SIZES]
    packed = jax.ShapeDtypeStruct((288, 512), bf16)
    return pl.pallas_call(
        delta_kernel,
        grid_spec=pltpu.PrefetchScalarGridSpec(
            num_scalar_prefetch=1,
            grid=(4,),
            in_specs=[whole(), whole(), whole()] + columns * 2,
            out_specs=[fixed((288, 512))] * 4 + [fixed((64, 8, 128))],
            scratch_shapes=[pltpu.VMEM((288, 128), f32)],
        ),
        out_shape=[packed] * 4 + [jax.ShapeDtypeStruct((64, 8, 128), f32)],
        cost_estimate=pl.CostEstimate(flops=4 * 288 * 1024 * 2048, bytes_accessed=12000000, transcendentals=0),
        name="deltas",
    )(place, keep, got, gain, *heads)


def combine_kernel(place_ref, sums_ref, a_ref, b_ref, c_ref, d_ref, out_ref):
    odd = lax.broadcasted_iota(jnp.int32, (32, 128), 0) % 2
    factors = []
    for h in range(2):
        rows = sums_ref[32 * h : 32 * h + 32, 0]
        for p in range(2):
            norm = jnp.sum(jnp.where(odd == p, rows, 0.0), axis=0, keepdims=True)
            factors.append(BOUND / jnp.maximum(jnp.sqrt(norm), BOUND))
    high_zero = place_ref[0] == 0
    core_zero = place_ref[2] == 0
    weights = []
    for d, c in SLOTS:
        pair = [jnp.where(high_zero, factors[2 * d + p], factors[2 - 2 * d + p]) for p in range(2)]
        weights.append(jnp.where(core_zero, pair[c], pair[1 - c]))
    refs = (a_ref, b_ref, c_ref, d_ref)

    def weighted(rows, lane):
        total = weights[0] * refs[0][rows, lane].astype(f32)
        for w, ref in zip(weights[1:], refs[1:]):
            total = total + w * ref[rows, lane].astype(f32)
        return total

    gain = jnp.zeros((3, 128), f32)
    for w, (d, c) in zip(weights, SLOTS):
        row = (place_ref[0] ^ d) * 32 + place_ref[1] * 16 + place_ref[3] * 2 + (place_ref[2] ^ c)
        gain = gain + w * sums_ref[row][1:4]
    high = gain.astype(bf16).astype(f32)
    extra = jnp.concatenate([high, gain - high, jnp.zeros((10, 128), f32)], axis=0).astype(bf16)
    left = lax.broadcasted_iota(jnp.int32, (144, 128), 1) < 64
    for j in range(4):
        part = weighted(slice(0, 288), slice(j * 128, j * 128 + 128))
        low, up = part[:144], part[144:]
        out_ref[2 * j, :144] = jnp.where(left, low, pltpu.roll(up, 64, 1)).astype(bf16)
        out_ref[2 * j + 1, :144] = jnp.where(left, pltpu.roll(low, 64, 1), up).astype(bf16)
        out_ref[2 * j, 144:] = extra
        out_ref[2 * j + 1, 144:] = extra


def combine(place, sums, parts):
    return pl.pallas_call(
        combine_kernel,
        in_specs=[place_spec()] + [whole()] * 5,
        out_specs=whole(),
        out_shape=jax.ShapeDtypeStruct((8, 160, 128), bf16),
        name="clip_and_combine",
    )(place, sums, *parts)


def finish_kernel(parts_ref, noise_ref, gain_noise_ref, out_ref, gain_ref):
    total = parts_ref[0].astype(f32)
    for i in range(1, 8):
        total = total + parts_ref[i].astype(f32)
    body = total[:144]
    rows = jnp.concatenate([body, pltpu.roll(body, 64, 1)], axis=0).T
    out_ref[...] = (rows[:64] + noise_ref[...]) * (1.0 / 32.0)
    gain_ref[...] = (total[144:147] + total[147:150] + gain_noise_ref[...]) * (1.0 / 32.0)


def finish(parts, noise, gain_noise):
    return pl.pallas_call(
        finish_kernel,
        out_shape=[jax.ShapeDtypeStruct((64, 288), f32), jax.ShapeDtypeStruct((3, 128), f32)],
        name="sum_and_noise",
    )(parts, noise, gain_noise)


def lanes(vector):
    return jnp.pad(vector, (0, 96)).reshape(3, 128)


def turn(x):
    return lax.ppermute(x, ("core", "xl"), [(0, 0), (1, 2), (2, 1), (3, 3)])


def along_y(x, step):
    return lax.ppermute(x, "y", [(i, (i + step) % 8) for i in range(8)])


def to_owner(x, flip_high, flip_core):
    pairs = []
    for h in range(2):
        for c in range(2):
            for p in range(2):
                pairs.append((h * 4 + c * 2 + p, (h ^ flip_high) * 4 + (p ^ flip_core) * 2 + c))
    return lax.ppermute(x, ("xh", "core", "xl"), pairs)


def local(head_outputs, out_weight, norm_gain, cotangent, loss_mask, weight_noise, gain_noise):
    xl = lax.axis_index("xl")
    core = lax.axis_index("core")
    place = jnp.stack([lax.axis_index("xh"), xl, core, lax.axis_index("y")]).astype(jnp.int32)
    masked = cotangent * loss_mask[:, None].astype(bf16)
    pieces = masked.reshape(128, 8, 2, 288).transpose(1, 2, 3, 0)
    low, high = pieces[:, 0], pieces[:, 1]
    ordered = jnp.concatenate(
        [jnp.where(xl == 0, low, high), jnp.where(xl == 0, high, low)], axis=1
    )
    ordered, turned = lax.optimization_barrier((ordered, turn(head_outputs)))
    arrived = lax.all_to_all(ordered, "y", split_axis=0, concat_axis=0, tiled=True)
    gain_got = swap(norm_gain, "xl")
    weight_t, gain_got, _ = lax.optimization_barrier((out_weight.T, gain_got, turned))
    weight_got = swap(weight_t, "xl")

    up, down = [turned], [turned]
    for _ in range(2):
        up.append(along_y(up[-1], 1))
        down.append(along_y(down[-1], -1))
    arrived, up[2], down[2], weight_got = lax.optimization_barrier((arrived, up[2], down[2], weight_got))
    arrived = turn(arrived)
    up.append(along_y(up[2], 1))
    down.append(along_y(down[2], -1))
    weight_t, weight_got, *blocks = lax.optimization_barrier((weight_t, weight_got, turned, up[1], down[1], up[2], down[2]))
    parts = [list(project(place, weight_t, weight_got, *x)) for x in (blocks[:3], blocks[3:])]
    parts[0][0], parts[1][0], up[3], down[3] = lax.optimization_barrier((parts[0][0], parts[1][0], up[3], down[3]))
    low, high = along_y(up[3][:64], 1), along_y(down[3][64:], -1)
    parts.append(project(place, weight_t, weight_got, up[3], down[3]))
    straight = xl == core
    gain = jnp.concatenate(
        [jnp.where(straight, norm_gain, gain_got), jnp.where(straight, gain_got, norm_gain)]
    )[:, None]
    sums = token_sums(place, [x[0] for x in parts], arrived, gain)
    sums, low, high = lax.optimization_barrier((sums, low, high))
    *last, stats = project_last(place, weight_t, weight_got, low, high, arrived, gain, sums)
    parts.append(last)
    projected, heads = [x[0] for x in parts], [x[1] for x in parts]
    others = [swap(x, "core") for x in heads]
    stats = lax.all_to_all(stats, "y", split_axis=0, concat_axis=0, tiled=True)
    keep_grad, send_grad, gain_keep = gradients(place, projected, arrived, gain, stats)
    got_grad = swap(send_grad, "core")
    *packed, squares = deltas(place, keep_grad, got_grad, gain_keep, *heads, *others)
    parts = [to_owner(x, *slot) for x, slot in zip(packed, SLOTS)]
    sums = lax.all_to_all(squares, ("xh", "core", "y", "xl"), split_axis=0, concat_axis=0, tiled=True)
    chip = combine(place, sums, parts)
    over_z = lax.all_to_all(chip, "z", split_axis=0, concat_axis=0, tiled=True)
    update, gain_update = finish(over_z, weight_noise, lanes(gain_noise))
    return update, gain_update.reshape(384)[:288]


def solution(mesh):
    split_mesh = Mesh(mesh.devices.reshape(2, 8, 2, 8, 2), CLIENT + FSDP)
    both = CLIENT + FSDP
    placed = (
        P(both, None),
        P(None, FSDP),
        P(FSDP),
        P(both, None),
        P(both),
        P(CLIENT, FSDP),
        P(FSDP),
    )
    return jax.shard_map(
        local,
        mesh=split_mesh,
        in_specs=placed,
        out_specs=(P(CLIENT, FSDP), P(FSDP)),
        check_vma=False,
    )
```

```python
import functools
import functools
import math

import jax
import jax.numpy as jnp
from jax import lax
from jax.experimental import pallas as pl
from jax.experimental.pallas import tpu as pltpu
from jax.sharding import Mesh, PartitionSpec as P

D = 4608
HD = 2048
epsilon = 1e-06
CLIENT = ("xh", "z", "core")
FSDP = ("y", "xl")
BOUND = math.sqrt(HD * D)
f32 = jnp.float32
bf16 = jnp.bfloat16


def swap(x, axis):
    return lax.ppermute(x, axis, [(0, 1), (1, 0)])


def full(shape):
    return pl.BlockSpec(shape, lambda *i: (0,) * len(shape))


def place_spec():
    return pl.BlockSpec(memory_space=pltpu.SMEM)


def whole():
    return pl.BlockSpec(memory_space=pltpu.VMEM)


SLOTS = ((1, 0), (0, 1), (0, 0), (1, 1))


def grad_kernel(sent, proj_ref, masked_ref, gain_ref, stats_ref, out_ref, *rest):
    total = rest[-1]
    step = pl.program_id(0)
    stats = stats_ref[0]
    for i in range(1, 8):
        stats = stats + stats_ref[i]
    inverse = lax.rsqrt(stats[0:1] / D + epsilon)
    coefficient = inverse * inverse * inverse * stats[1:2] / D

    def part(first):
        for start in range(0, 144, 48):
            rows = slice(start, start + 48)
            gain = jnp.broadcast_to(gain_ref[rows], (48, 128))
            summed = jnp.zeros((48, 128), f32)
            for i in range(8):
                lane = slice(128 * i, 128 * i + 128)
                p = proj_ref[rows, lane]
                m = masked_ref[i, rows].astype(f32) * inverse[:, lane]
                out_ref[first + start : first + start + 48, lane] = (gain * m - p * coefficient[:, lane]).astype(bf16)
                summed += m * p
            total[first + start : first + start + 48] = summed

    for n in range(2):

        @pl.when(step == n)
        def _(n=n):
            part(144 * n)

    @pl.when(step == 1)
    def _():
        row = jnp.sum(total[...].T, axis=0, keepdims=True)
        row = jnp.concatenate([row, jnp.zeros((1, 96), f32)], axis=1)
        gain = jnp.concatenate([row[:, 0:128], row[:, 128:256], row[:, 256:384]], axis=0)
        if sent:
            high = gain.astype(bf16).astype(f32)
            extra = jnp.concatenate([high, gain - high, jnp.zeros((10, 128), f32)], axis=0).astype(bf16)
            for i in range(8):
                out_ref[288:, 128 * i : 128 * i + 128] = extra
        else:
            rest[0][...] = gain


def gradients(sent, projected, masked, gain, stats):
    base = 2 if sent else 0
    rows = 304 if sent else 288
    outs = [((rows, 1024), bf16)] + ([] if sent else [((3, 128), f32)])
    return pl.pallas_call(
        functools.partial(grad_kernel, sent),
        grid=(2,),
        in_specs=[
            pl.BlockSpec((144, 1024), lambda n: (base + n, 0)),
            pl.BlockSpec((8, 144, 128), lambda n: (0, base + n, 0)),
            pl.BlockSpec((144, 1), lambda n: (base + n, 0)),
            full((8, 2, 1024)),
        ],
        out_specs=[full(shape) for shape, _ in outs],
        out_shape=[jax.ShapeDtypeStruct(shape, kind) for shape, kind in outs],
        scratch_shapes=[pltpu.VMEM((288, 128), f32)],
        cost_estimate=pl.CostEstimate(flops=4000000, bytes_accessed=6000000, transcendentals=0),
        name="gradients_sent" if sent else "gradients_kept",
    )(projected, masked, gain, stats)


def delta_kernel(place_ref, keep_ref, got_ref, gain_ref, heads_ref, other_ref, *rest):
    outs, sum_ref, total = rest[:4], rest[4], rest[5]
    step = pl.program_id(0)
    value = jnp.dot(keep_ref[...], heads_ref[...], preferred_element_type=f32)
    value = value + jnp.dot(got_ref[:288], other_ref[...], preferred_element_type=f32)
    folded = jnp.zeros((288, 128), f32)
    for j in range(8):
        folded += value[:, 128 * j : 128 * j + 128] * value[:, 128 * j : 128 * j + 128]
    left = lax.broadcasted_iota(jnp.int32, (288, 128), 1) < 64
    zero = place_ref[1] == 0

    def pack(d):
        for j in range(4):
            a, b = value[:, 256 * j : 256 * j + 128], value[:, 256 * j + 128 : 256 * j + 256]
            first = jnp.where(left, a, pltpu.roll(b, 64, 1))
            second = jnp.where(left, pltpu.roll(a, 64, 1), b)
            lane = slice(j * 128, j * 128 + 128)
            outs[SLOTS.index((d, 0))][:, lane] = jnp.where(zero, first, second).astype(bf16)
            outs[SLOTS.index((d, 1))][:, lane] = jnp.where(zero, second, first).astype(bf16)

    @pl.when(step == 0)
    def _():
        total[...] = folded
        pack(1)

    @pl.when(step == 1)
    def _():
        total[...] += folded
        pack(0)

    @pl.when(step == 1)
    def _():
        extra = got_ref[288:, :128].astype(f32)
        gain = gain_ref[...] + extra[0:3] + extra[3:6]
        norm = jnp.sum(total[...]) + jnp.sum(gain * gain)
        tile = jnp.concatenate([jnp.full((1, 128), norm, f32), gain, jnp.zeros((4, 128), f32)], axis=0)
        for i in range(64):
            sum_ref[i] = tile


def deltas(place, keep, got, gain, heads, other_heads):
    fixed = lambda shape: pl.BlockSpec(shape, lambda n, place: (0,) * len(shape))
    columns = pl.BlockSpec((1024, 1024), lambda n, place: (0, place[0] ^ (1 - n)))
    packed = jax.ShapeDtypeStruct((288, 512), bf16)
    return pl.pallas_call(
        delta_kernel,
        grid_spec=pltpu.PrefetchScalarGridSpec(
            num_scalar_prefetch=1,
            grid=(2,),
            in_specs=[whole(), whole(), whole(), columns, columns],
            out_specs=[fixed((288, 512))] * 4 + [fixed((64, 8, 128))],
            scratch_shapes=[pltpu.VMEM((288, 128), f32)],
        ),
        out_shape=[packed] * 4 + [jax.ShapeDtypeStruct((64, 8, 128), f32)],
        cost_estimate=pl.CostEstimate(flops=4 * 288 * 1024 * 2048, bytes_accessed=12000000, transcendentals=0),
        compiler_params=pltpu.CompilerParams(vmem_limit_bytes=32 * 2**20),
        name="deltas",
    )(place, keep, got, gain, heads, other_heads)


def combine_kernel(place_ref, sums_ref, a_ref, b_ref, c_ref, d_ref, out_ref):
    odd = lax.broadcasted_iota(jnp.int32, (32, 128), 0) % 2
    factors = []
    for h in range(2):
        rows = sums_ref[32 * h : 32 * h + 32, 0]
        for p in range(2):
            norm = jnp.sum(jnp.where(odd == p, rows, 0.0), axis=0, keepdims=True)
            factors.append(BOUND / jnp.maximum(jnp.sqrt(norm), BOUND))
    high_zero = place_ref[0] == 0
    core_zero = place_ref[2] == 0
    weights = []
    for d, c in SLOTS:
        pair = [jnp.where(high_zero, factors[2 * d + p], factors[2 - 2 * d + p]) for p in range(2)]
        weights.append(jnp.where(core_zero, pair[c], pair[1 - c]))
    refs = (a_ref, b_ref, c_ref, d_ref)

    def weighted(rows, lane):
        total = weights[0] * refs[0][rows, lane].astype(f32)
        for w, ref in zip(weights[1:], refs[1:]):
            total = total + w * ref[rows, lane].astype(f32)
        return total

    gain = jnp.zeros((3, 128), f32)
    for w, (d, c) in zip(weights, SLOTS):
        row = (place_ref[0] ^ d) * 32 + place_ref[1] * 16 + place_ref[3] * 2 + (place_ref[2] ^ c)
        gain = gain + w * sums_ref[row][1:4]
    high = gain.astype(bf16).astype(f32)
    extra = jnp.concatenate([high, gain - high, jnp.zeros((10, 128), f32)], axis=0).astype(bf16)
    left = lax.broadcasted_iota(jnp.int32, (144, 128), 1) < 64
    for j in range(4):
        part = weighted(slice(0, 288), slice(j * 128, j * 128 + 128))
        low, up = part[:144], part[144:]
        out_ref[2 * j, :144] = jnp.where(left, low, pltpu.roll(up, 64, 1)).astype(bf16)
        out_ref[2 * j + 1, :144] = jnp.where(left, pltpu.roll(low, 64, 1), up).astype(bf16)
        out_ref[2 * j, 144:] = extra
        out_ref[2 * j + 1, 144:] = extra


def combine(place, sums, parts):
    return pl.pallas_call(
        combine_kernel,
        in_specs=[place_spec()] + [whole()] * 5,
        out_specs=whole(),
        out_shape=jax.ShapeDtypeStruct((8, 160, 128), bf16),
        name="clip_and_combine",
    )(place, sums, *parts)


def finish_kernel(parts_ref, noise_ref, gain_noise_ref, out_ref, gain_ref):
    total = parts_ref[0].astype(f32)
    for i in range(1, 8):
        total = total + parts_ref[i].astype(f32)
    body = total[:144]
    rows = jnp.concatenate([body, pltpu.roll(body, 64, 1)], axis=0).T
    out_ref[...] = (rows[:64] + noise_ref[...]) * (1.0 / 32.0)
    gain_ref[...] = (total[144:147] + total[147:150] + gain_noise_ref[...]) * (1.0 / 32.0)


def finish(parts, noise, gain_noise):
    return pl.pallas_call(
        finish_kernel,
        out_shape=[jax.ShapeDtypeStruct((64, 288), f32), jax.ShapeDtypeStruct((3, 128), f32)],
        name="sum_and_noise",
    )(parts, noise, gain_noise)


def lanes(vector):
    return jnp.pad(vector, (0, 96)).reshape(3, 128)


def turn(x):
    return lax.ppermute(x, ("core", "xl"), [(0, 0), (1, 2), (2, 1), (3, 3)])


def to_owner(x, flip_high, flip_core):
    pairs = []
    for h in range(2):
        for c in range(2):
            for p in range(2):
                pairs.append((h * 4 + c * 2 + p, (h ^ flip_high) * 4 + (p ^ flip_core) * 2 + c))
    return lax.ppermute(x, ("xh", "core", "xl"), pairs)


def local(head_outputs, out_weight, norm_gain, cotangent, loss_mask, weight_noise, gain_noise):
    xl = lax.axis_index("xl")
    core = lax.axis_index("core")
    place = jnp.stack([lax.axis_index("xh"), xl, core, lax.axis_index("y")]).astype(jnp.int32)
    turned = turn(head_outputs)
    heads = lax.all_gather(turned, "y", axis=0, tiled=True)
    masked = cotangent * loss_mask[:, None].astype(bf16)
    pieces = masked.reshape(128, 8, 2, 288).transpose(1, 2, 3, 0)
    low, high = pieces[:, 0], pieces[:, 1]
    ordered = jnp.concatenate(
        [jnp.where(xl == 0, low, high), jnp.where(xl == 0, high, low)], axis=1
    )
    arrived = turn(lax.all_to_all(ordered, "y", split_axis=0, concat_axis=0, tiled=True))
    weight_t, own_gain, _ = lax.optimization_barrier((out_weight.T, norm_gain, turned))
    weight_got, gain_got = swap(weight_t, "xl"), swap(own_gain, "xl")
    straight = xl == core
    weights = jnp.concatenate(
        [jnp.where(straight, weight_t, weight_got), jnp.where(straight, weight_got, weight_t)], axis=0
    )
    gain = jnp.concatenate(
        [jnp.where(straight, own_gain, gain_got), jnp.where(straight, gain_got, own_gain)]
    )
    heads, weights, arrived, gain = lax.optimization_barrier((heads, weights, arrived, gain))
    gain = gain[:, None]
    other_heads = swap(heads, "core")
    cotangents = arrived.transpose(1, 0, 2).reshape(576, 1024).astype(f32)
    projected = lax.dot_general(
        weights, heads, (((1,), (1,)), ((), ())), preferred_element_type=f32
    )
    stats = jnp.stack(
        [jnp.sum(projected * projected, axis=0), jnp.sum(projected * gain * cotangents, axis=0)]
    )
    stats = lax.all_to_all(
        jnp.broadcast_to(stats[None], (8, 2, 1024)), "y", split_axis=0, concat_axis=0, tiled=True
    )
    got_grad = swap(gradients(True, projected, arrived, gain, stats)[0], "core")
    keep_grad, gain_keep = gradients(False, projected, arrived, gain, stats)
    *packed, squares = deltas(place, keep_grad, got_grad, gain_keep, heads, other_heads)
    parts = [to_owner(x, *slot) for x, slot in zip(packed, SLOTS)]
    sums = lax.all_to_all(squares, ("xh", "core", "y", "xl"), split_axis=0, concat_axis=0, tiled=True)
    chip = combine(place, sums, parts)
    over_z = lax.all_to_all(chip, "z", split_axis=0, concat_axis=0, tiled=True)
    update, gain_update = finish(over_z, weight_noise, lanes(gain_noise))
    return update, gain_update.reshape(384)[:288]


def solution(mesh):
    split_mesh = Mesh(mesh.devices.reshape(2, 8, 2, 8, 2), CLIENT + FSDP)
    both = CLIENT + FSDP
    placed = (
        P(both, None),
        P(None, FSDP),
        P(FSDP),
        P(both, None),
        P(both),
        P(CLIENT, FSDP),
        P(FSDP),
    )
    return jax.shard_map(
        local,
        mesh=split_mesh,
        in_specs=placed,
        out_specs=(P(CLIENT, FSDP), P(FSDP)),
        check_vma=False,
    )
```

```python
import functools
import functools
import math

import jax
import jax.numpy as jnp
from jax import lax
from jax.experimental import pallas as pl
from jax.experimental.pallas import tpu as pltpu
from jax.sharding import Mesh, PartitionSpec as P

D = 4608
HD = 2048
epsilon = 1e-06
CLIENT = ("xh", "z", "core")
FSDP = ("y", "xl")
BOUND = math.sqrt(HD * D)
f32 = jnp.float32
bf16 = jnp.bfloat16


def swap(x, axis):
    return lax.ppermute(x, axis, [(0, 1), (1, 0)])


def full(shape):
    return pl.BlockSpec(shape, lambda *i: (0,) * len(shape))


def place_spec():
    return pl.BlockSpec(memory_space=pltpu.SMEM)


def whole():
    return pl.BlockSpec(memory_space=pltpu.VMEM)


SLOTS = ((1, 0), (1, 1), (0, 0), (0, 1))


def grad_kernel(sent, proj_ref, masked_ref, gain_ref, stats_ref, out_ref, *rest):
    total = rest[-1]
    step = pl.program_id(0)
    stats = stats_ref[0]
    for i in range(1, 8):
        stats = stats + stats_ref[i]
    inverse = lax.rsqrt(stats[0:1] / D + epsilon)
    coefficient = inverse * inverse * inverse * stats[1:2] / D

    def part(first):
        for start in range(0, 144, 48):
            rows = slice(start, start + 48)
            gain = jnp.broadcast_to(gain_ref[rows], (48, 128))
            summed = jnp.zeros((48, 128), f32)
            for i in range(8):
                lane = slice(128 * i, 128 * i + 128)
                p = proj_ref[rows, lane]
                m = masked_ref[i, rows].astype(f32) * inverse[:, lane]
                out_ref[first + start : first + start + 48, lane] = (gain * m - p * coefficient[:, lane]).astype(bf16)
                summed += m * p
            total[first + start : first + start + 48] = summed

    for n in range(2):

        @pl.when(step == n)
        def _(n=n):
            part(144 * n)

    @pl.when(step == 1)
    def _():
        row = jnp.sum(total[...].T, axis=0, keepdims=True)
        row = jnp.concatenate([row, jnp.zeros((1, 96), f32)], axis=1)
        gain = jnp.concatenate([row[:, 0:128], row[:, 128:256], row[:, 256:384]], axis=0)
        if sent:
            high = gain.astype(bf16).astype(f32)
            extra = jnp.concatenate([high, gain - high, jnp.zeros((10, 128), f32)], axis=0).astype(bf16)
            for i in range(8):
                out_ref[288:, 128 * i : 128 * i + 128] = extra
        else:
            rest[0][...] = gain


def gradients(sent, projected, masked, gain, stats):
    base = 2 if sent else 0
    rows = 304 if sent else 288
    outs = [((rows, 1024), bf16)] + ([] if sent else [((3, 128), f32)])
    return pl.pallas_call(
        functools.partial(grad_kernel, sent),
        grid=(2,),
        in_specs=[
            pl.BlockSpec((144, 1024), lambda n: (base + n, 0)),
            pl.BlockSpec((8, 144, 128), lambda n: (0, base + n, 0)),
            pl.BlockSpec((144, 1), lambda n: (base + n, 0)),
            full((8, 2, 1024)),
        ],
        out_specs=[full(shape) for shape, _ in outs],
        out_shape=[jax.ShapeDtypeStruct(shape, kind) for shape, kind in outs],
        scratch_shapes=[pltpu.VMEM((288, 128), f32)],
        cost_estimate=pl.CostEstimate(flops=4000000, bytes_accessed=6000000, transcendentals=0),
        name="gradients_sent" if sent else "gradients_kept",
    )(projected, masked, gain, stats)


def delta_kernel(place_ref, keep_ref, got_ref, gain_ref, heads_ref, other_ref, *rest):
    outs, sum_ref, total = rest[:4], rest[4], rest[5]
    step = pl.program_id(0)
    value = jnp.dot(keep_ref[...], heads_ref[...], preferred_element_type=f32)
    value = value + jnp.dot(got_ref[:288], other_ref[...], preferred_element_type=f32)
    folded = jnp.zeros((288, 128), f32)
    for j in range(8):
        folded += value[:, 128 * j : 128 * j + 128] * value[:, 128 * j : 128 * j + 128]
    left = lax.broadcasted_iota(jnp.int32, (288, 128), 1) < 64
    zero = place_ref[1] == 0

    def pack(d):
        for j in range(4):
            a, b = value[:, 256 * j : 256 * j + 128], value[:, 256 * j + 128 : 256 * j + 256]
            first = jnp.where(left, a, pltpu.roll(b, 64, 1))
            second = jnp.where(left, pltpu.roll(a, 64, 1), b)
            lane = slice(j * 128, j * 128 + 128)
            outs[SLOTS.index((d, 0))][:, lane] = jnp.where(zero, first, second).astype(bf16)
            outs[SLOTS.index((d, 1))][:, lane] = jnp.where(zero, second, first).astype(bf16)

    @pl.when(step == 0)
    def _():
        total[...] = folded
        pack(1)

    @pl.when(step == 1)
    def _():
        total[...] += folded
        pack(0)

    @pl.when(step == 1)
    def _():
        extra = got_ref[288:, :128].astype(f32)
        gain = gain_ref[...] + extra[0:3] + extra[3:6]
        norm = jnp.sum(total[...]) + jnp.sum(gain * gain)
        tile = jnp.concatenate([jnp.full((1, 128), norm, f32), gain, jnp.zeros((4, 128), f32)], axis=0)
        for i in range(64):
            sum_ref[i] = tile


def deltas(place, keep, got, gain, heads, other_heads):
    fixed = lambda shape: pl.BlockSpec(shape, lambda n, place: (0,) * len(shape))
    columns = pl.BlockSpec((1024, 1024), lambda n, place: (0, place[0] ^ (1 - n)))
    packed = jax.ShapeDtypeStruct((288, 512), bf16)
    return pl.pallas_call(
        delta_kernel,
        grid_spec=pltpu.PrefetchScalarGridSpec(
            num_scalar_prefetch=1,
            grid=(2,),
            in_specs=[whole(), whole(), whole(), columns, columns],
            out_specs=[fixed((288, 512))] * 4 + [fixed((64, 8, 128))],
            scratch_shapes=[pltpu.VMEM((288, 128), f32)],
        ),
        out_shape=[packed] * 4 + [jax.ShapeDtypeStruct((64, 8, 128), f32)],
        cost_estimate=pl.CostEstimate(flops=4 * 288 * 1024 * 2048, bytes_accessed=12000000, transcendentals=0),
        name="deltas",
    )(place, keep, got, gain, heads, other_heads)


def combine_kernel(place_ref, sums_ref, a_ref, b_ref, c_ref, d_ref, out_ref):
    odd = lax.broadcasted_iota(jnp.int32, (32, 128), 0) % 2
    factors = []
    for h in range(2):
        rows = sums_ref[32 * h : 32 * h + 32, 0]
        for p in range(2):
            norm = jnp.sum(jnp.where(odd == p, rows, 0.0), axis=0, keepdims=True)
            factors.append(BOUND / jnp.maximum(jnp.sqrt(norm), BOUND))
    high_zero = place_ref[0] == 0
    core_zero = place_ref[2] == 0
    weights = []
    for d, c in SLOTS:
        pair = [jnp.where(high_zero, factors[2 * d + p], factors[2 - 2 * d + p]) for p in range(2)]
        weights.append(jnp.where(core_zero, pair[c], pair[1 - c]))
    refs = (a_ref, b_ref, c_ref, d_ref)

    def weighted(rows, lane):
        total = weights[0] * refs[0][rows, lane].astype(f32)
        for w, ref in zip(weights[1:], refs[1:]):
            total = total + w * ref[rows, lane].astype(f32)
        return total

    gain = jnp.zeros((3, 128), f32)
    for w, (d, c) in zip(weights, SLOTS):
        row = (place_ref[0] ^ d) * 32 + place_ref[1] * 16 + place_ref[3] * 2 + (place_ref[2] ^ c)
        gain = gain + w * sums_ref[row][1:4]
    high = gain.astype(bf16).astype(f32)
    extra = jnp.concatenate([high, gain - high, jnp.zeros((10, 128), f32)], axis=0).astype(bf16)
    left = lax.broadcasted_iota(jnp.int32, (144, 128), 1) < 64
    for j in range(4):
        part = weighted(slice(0, 288), slice(j * 128, j * 128 + 128))
        low, up = part[:144], part[144:]
        out_ref[2 * j, :144] = jnp.where(left, low, pltpu.roll(up, 64, 1)).astype(bf16)
        out_ref[2 * j + 1, :144] = jnp.where(left, pltpu.roll(low, 64, 1), up).astype(bf16)
        out_ref[2 * j, 144:] = extra
        out_ref[2 * j + 1, 144:] = extra


def combine(place, sums, parts):
    return pl.pallas_call(
        combine_kernel,
        in_specs=[place_spec()] + [whole()] * 5,
        out_specs=whole(),
        out_shape=jax.ShapeDtypeStruct((8, 160, 128), bf16),
        name="clip_and_combine",
    )(place, sums, *parts)


def finish_kernel(parts_ref, noise_ref, gain_noise_ref, out_ref, gain_ref):
    total = parts_ref[0].astype(f32)
    for i in range(1, 8):
        total = total + parts_ref[i].astype(f32)
    body = total[:144]
    rows = jnp.concatenate([body, pltpu.roll(body, 64, 1)], axis=0).T
    out_ref[...] = (rows[:64] + noise_ref[...]) * (1.0 / 32.0)
    gain_ref[...] = (total[144:147] + total[147:150] + gain_noise_ref[...]) * (1.0 / 32.0)


def finish(parts, noise, gain_noise):
    return pl.pallas_call(
        finish_kernel,
        out_shape=[jax.ShapeDtypeStruct((64, 288), f32), jax.ShapeDtypeStruct((3, 128), f32)],
        name="sum_and_noise",
    )(parts, noise, gain_noise)


def lanes(vector):
    return jnp.pad(vector, (0, 96)).reshape(3, 128)


def turn(x):
    return lax.ppermute(x, ("core", "xl"), [(0, 0), (1, 2), (2, 1), (3, 3)])


def to_owner(x, flip_high, flip_core):
    pairs = []
    for h in range(2):
        for c in range(2):
            for p in range(2):
                pairs.append((h * 4 + c * 2 + p, (h ^ flip_high) * 4 + (p ^ flip_core) * 2 + c))
    return lax.ppermute(x, ("xh", "core", "xl"), pairs)


def local(head_outputs, out_weight, norm_gain, cotangent, loss_mask, weight_noise, gain_noise):
    xl = lax.axis_index("xl")
    core = lax.axis_index("core")
    place = jnp.stack([lax.axis_index("xh"), xl, core, lax.axis_index("y")]).astype(jnp.int32)
    turned = turn(head_outputs)
    heads = lax.all_gather(turned, "y", axis=0, tiled=True)
    masked = cotangent * loss_mask[:, None].astype(bf16)
    pieces = masked.reshape(128, 8, 2, 288).transpose(1, 2, 3, 0)
    low, high = pieces[:, 0], pieces[:, 1]
    ordered = jnp.concatenate(
        [jnp.where(xl == 0, low, high), jnp.where(xl == 0, high, low)], axis=1
    )
    arrived = turn(lax.all_to_all(ordered, "y", split_axis=0, concat_axis=0, tiled=True))
    weight_t, own_gain, _ = lax.optimization_barrier((out_weight.T, norm_gain, turned))
    weight_got, gain_got = swap(weight_t, "xl"), swap(own_gain, "xl")
    straight = xl == core
    weights = jnp.concatenate(
        [jnp.where(straight, weight_t, weight_got), jnp.where(straight, weight_got, weight_t)], axis=0
    )
    gain = jnp.concatenate(
        [jnp.where(straight, own_gain, gain_got), jnp.where(straight, gain_got, own_gain)]
    )
    heads, weights, arrived, gain = lax.optimization_barrier((heads, weights, arrived, gain))
    gain = gain[:, None]
    other_heads = swap(heads, "core")
    cotangents = arrived.transpose(1, 0, 2).reshape(576, 1024).astype(f32)
    projected = lax.dot_general(
        weights, heads, (((1,), (1,)), ((), ())), preferred_element_type=f32
    )
    stats = jnp.stack(
        [jnp.sum(projected * projected, axis=0), jnp.sum(projected * gain * cotangents, axis=0)]
    )
    stats = lax.all_to_all(
        jnp.broadcast_to(stats[None], (8, 2, 1024)), "y", split_axis=0, concat_axis=0, tiled=True
    )
    got_grad = swap(gradients(True, projected, arrived, gain, stats)[0], "core")
    keep_grad, gain_keep = gradients(False, projected, arrived, gain, stats)
    *packed, squares = deltas(place, keep_grad, got_grad, gain_keep, heads, other_heads)
    parts = [to_owner(x, *slot) for x, slot in zip(packed, SLOTS)]
    sums = lax.all_to_all(squares, ("xh", "core", "y", "xl"), split_axis=0, concat_axis=0, tiled=True)
    chip = combine(place, sums, parts)
    over_z = lax.all_to_all(chip, "z", split_axis=0, concat_axis=0, tiled=True)
    update, gain_update = finish(over_z, weight_noise, lanes(gain_noise))
    return update, gain_update.reshape(384)[:288]


def solution(mesh):
    split_mesh = Mesh(mesh.devices.reshape(2, 8, 2, 8, 2), CLIENT + FSDP)
    both = CLIENT + FSDP
    placed = (
        P(both, None),
        P(None, FSDP),
        P(FSDP),
        P(both, None),
        P(both),
        P(CLIENT, FSDP),
        P(FSDP),
    )
    return jax.shard_map(
        local,
        mesh=split_mesh,
        in_specs=placed,
        out_specs=(P(CLIENT, FSDP), P(FSDP)),
        check_vma=False,
    )
```

```python
import functools
import functools
import math

import jax
import jax.numpy as jnp
from jax import lax
from jax.experimental import pallas as pl
from jax.experimental.pallas import tpu as pltpu
from jax.sharding import Mesh, PartitionSpec as P

D = 4608
HD = 2048
epsilon = 1e-06
CLIENT = ("xh", "z", "core")
FSDP = ("y", "xl")
BOUND = math.sqrt(HD * D)
f32 = jnp.float32
bf16 = jnp.bfloat16


def swap(x, axis):
    return lax.ppermute(x, axis, [(0, 1), (1, 0)])


def full(shape):
    return pl.BlockSpec(shape, lambda *i: (0,) * len(shape))


def place_spec():
    return pl.BlockSpec(memory_space=pltpu.SMEM)


def whole():
    return pl.BlockSpec(memory_space=pltpu.VMEM)


SLOTS = ((1, 0), (1, 1), (0, 0), (0, 1))


def grad_kernel(sent, proj_ref, masked_ref, gain_ref, stats_ref, out_ref, *rest):
    total = rest[-1]
    step = pl.program_id(0)
    stats = stats_ref[0]
    for i in range(1, 8):
        stats = stats + stats_ref[i]
    inverse = lax.rsqrt(stats[0:1] / D + epsilon)
    coefficient = inverse * inverse * inverse * stats[1:2] / D

    def part(first):
        for start in range(0, 144, 48):
            rows = slice(start, start + 48)
            gain = jnp.broadcast_to(gain_ref[rows], (48, 128))
            summed = jnp.zeros((48, 128), f32)
            for i in range(8):
                lane = slice(128 * i, 128 * i + 128)
                p = proj_ref[rows, lane]
                m = masked_ref[i, rows].astype(f32) * inverse[:, lane]
                out_ref[first + start : first + start + 48, lane] = (gain * m - p * coefficient[:, lane]).astype(bf16)
                summed += m * p
            total[first + start : first + start + 48] = summed

    for n in range(2):

        @pl.when(step == n)
        def _(n=n):
            part(144 * n)

    @pl.when(step == 1)
    def _():
        row = jnp.sum(total[...].T, axis=0, keepdims=True)
        row = jnp.concatenate([row, jnp.zeros((1, 96), f32)], axis=1)
        gain = jnp.concatenate([row[:, 0:128], row[:, 128:256], row[:, 256:384]], axis=0)
        if sent:
            high = gain.astype(bf16).astype(f32)
            extra = jnp.concatenate([high, gain - high, jnp.zeros((10, 128), f32)], axis=0).astype(bf16)
            for i in range(8):
                out_ref[288:, 128 * i : 128 * i + 128] = extra
        else:
            rest[0][...] = gain


def gradients(sent, projected, masked, gain, stats):
    base = 2 if sent else 0
    rows = 304 if sent else 288
    outs = [((rows, 1024), bf16)] + ([] if sent else [((3, 128), f32)])
    return pl.pallas_call(
        functools.partial(grad_kernel, sent),
        grid=(2,),
        in_specs=[
            pl.BlockSpec((144, 1024), lambda n: (base + n, 0)),
            pl.BlockSpec((8, 144, 128), lambda n: (0, base + n, 0)),
            pl.BlockSpec((144, 1), lambda n: (base + n, 0)),
            full((8, 2, 1024)),
        ],
        out_specs=[full(shape) for shape, _ in outs],
        out_shape=[jax.ShapeDtypeStruct(shape, kind) for shape, kind in outs],
        scratch_shapes=[pltpu.VMEM((288, 128), f32)],
        cost_estimate=pl.CostEstimate(flops=4000000, bytes_accessed=6000000, transcendentals=0),
        name="gradients_sent" if sent else "gradients_kept",
    )(projected, masked, gain, stats)


def delta_kernel(place_ref, keep_ref, got_ref, gain_ref, heads_ref, other_ref, *rest):
    outs, sum_ref, total = rest[:4], rest[4], rest[5]
    step = pl.program_id(0)
    value = jnp.dot(keep_ref[...], heads_ref[...], preferred_element_type=f32)
    value = value + jnp.dot(got_ref[:288], other_ref[...], preferred_element_type=f32)
    folded = jnp.zeros((288, 128), f32)
    for j in range(8):
        folded += value[:, 128 * j : 128 * j + 128] * value[:, 128 * j : 128 * j + 128]
    left = lax.broadcasted_iota(jnp.int32, (288, 128), 1) < 64
    zero = place_ref[1] == 0

    def pack(d):
        for j in range(4):
            a, b = value[:, 256 * j : 256 * j + 128], value[:, 256 * j + 128 : 256 * j + 256]
            first = jnp.where(left, a, pltpu.roll(b, 64, 1))
            second = jnp.where(left, pltpu.roll(a, 64, 1), b)
            lane = slice(j * 128, j * 128 + 128)
            outs[SLOTS.index((d, 0))][:, lane] = jnp.where(zero, first, second).astype(bf16)
            outs[SLOTS.index((d, 1))][:, lane] = jnp.where(zero, second, first).astype(bf16)

    @pl.when(step == 0)
    def _():
        total[...] = folded
        pack(1)

    @pl.when(step == 1)
    def _():
        total[...] += folded
        pack(0)

    @pl.when(step == 1)
    def _():
        extra = got_ref[288:, :128].astype(f32)
        gain = gain_ref[...] + extra[0:3] + extra[3:6]
        norm = jnp.sum(total[...]) + jnp.sum(gain * gain)
        tile = jnp.concatenate([jnp.full((1, 128), norm, f32), gain], axis=0)
        for i in range(64):
            sum_ref[i] = tile


def deltas(place, keep, got, gain, heads, other_heads):
    fixed = lambda shape: pl.BlockSpec(shape, lambda n, place: (0,) * len(shape))
    columns = pl.BlockSpec((1024, 1024), lambda n, place: (0, place[0] ^ (1 - n)))
    packed = jax.ShapeDtypeStruct((288, 512), bf16)
    return pl.pallas_call(
        delta_kernel,
        grid_spec=pltpu.PrefetchScalarGridSpec(
            num_scalar_prefetch=1,
            grid=(2,),
            in_specs=[whole(), whole(), whole(), columns, columns],
            out_specs=[fixed((288, 512))] * 4 + [fixed((64, 4, 128))],
            scratch_shapes=[pltpu.VMEM((288, 128), f32)],
        ),
        out_shape=[packed] * 4 + [jax.ShapeDtypeStruct((64, 4, 128), f32)],
        cost_estimate=pl.CostEstimate(flops=4 * 288 * 1024 * 2048, bytes_accessed=12000000, transcendentals=0),
        name="deltas",
    )(place, keep, got, gain, heads, other_heads)


def combine_kernel(place_ref, sums_ref, a_ref, b_ref, c_ref, d_ref, out_ref):
    odd = lax.broadcasted_iota(jnp.int32, (32, 128), 0) % 2
    factors = []
    for h in range(2):
        rows = sums_ref[32 * h : 32 * h + 32, 0]
        for p in range(2):
            norm = jnp.sum(jnp.where(odd == p, rows, 0.0), axis=0, keepdims=True)
            factors.append(BOUND / jnp.maximum(jnp.sqrt(norm), BOUND))
    high_zero = place_ref[0] == 0
    core_zero = place_ref[2] == 0
    weights = []
    for d, c in SLOTS:
        pair = [jnp.where(high_zero, factors[2 * d + p], factors[2 - 2 * d + p]) for p in range(2)]
        weights.append(jnp.where(core_zero, pair[c], pair[1 - c]))
    refs = (a_ref, b_ref, c_ref, d_ref)

    def weighted(rows, lane):
        total = weights[0] * refs[0][rows, lane].astype(f32)
        for w, ref in zip(weights[1:], refs[1:]):
            total = total + w * ref[rows, lane].astype(f32)
        return total

    gain = jnp.zeros((3, 128), f32)
    for w, (d, c) in zip(weights, SLOTS):
        row = (place_ref[0] ^ d) * 32 + place_ref[1] * 16 + place_ref[3] * 2 + (place_ref[2] ^ c)
        gain = gain + w * sums_ref[row][1:4]
    high = gain.astype(bf16).astype(f32)
    extra = jnp.concatenate([high, gain - high, jnp.zeros((10, 128), f32)], axis=0).astype(bf16)
    left = lax.broadcasted_iota(jnp.int32, (144, 128), 1) < 64
    for j in range(4):
        part = weighted(slice(0, 288), slice(j * 128, j * 128 + 128))
        low, up = part[:144], part[144:]
        out_ref[2 * j, :144] = jnp.where(left, low, pltpu.roll(up, 64, 1)).astype(bf16)
        out_ref[2 * j + 1, :144] = jnp.where(left, pltpu.roll(low, 64, 1), up).astype(bf16)
        out_ref[2 * j, 144:] = extra
        out_ref[2 * j + 1, 144:] = extra


def combine(place, sums, parts):
    return pl.pallas_call(
        combine_kernel,
        in_specs=[place_spec()] + [whole()] * 5,
        out_specs=whole(),
        out_shape=jax.ShapeDtypeStruct((8, 160, 128), bf16),
        name="clip_and_combine",
    )(place, sums, *parts)


def finish_kernel(parts_ref, noise_ref, gain_noise_ref, out_ref, gain_ref):
    total = parts_ref[0].astype(f32)
    for i in range(1, 8):
        total = total + parts_ref[i].astype(f32)
    body = total[:144]
    rows = jnp.concatenate([body, pltpu.roll(body, 64, 1)], axis=0).T
    out_ref[...] = (rows[:64] + noise_ref[...]) * (1.0 / 32.0)
    gain_ref[...] = (total[144:147] + total[147:150] + gain_noise_ref[...]) * (1.0 / 32.0)


def finish(parts, noise, gain_noise):
    return pl.pallas_call(
        finish_kernel,
        out_shape=[jax.ShapeDtypeStruct((64, 288), f32), jax.ShapeDtypeStruct((3, 128), f32)],
        name="sum_and_noise",
    )(parts, noise, gain_noise)


def lanes(vector):
    return jnp.pad(vector, (0, 96)).reshape(3, 128)


def turn(x):
    return lax.ppermute(x, ("core", "xl"), [(0, 0), (1, 2), (2, 1), (3, 3)])


def to_owner(x, flip_high, flip_core):
    pairs = []
    for h in range(2):
        for c in range(2):
            for p in range(2):
                pairs.append((h * 4 + c * 2 + p, (h ^ flip_high) * 4 + (p ^ flip_core) * 2 + c))
    return lax.ppermute(x, ("xh", "core", "xl"), pairs)


def local(head_outputs, out_weight, norm_gain, cotangent, loss_mask, weight_noise, gain_noise):
    xl = lax.axis_index("xl")
    core = lax.axis_index("core")
    place = jnp.stack([lax.axis_index("xh"), xl, core, lax.axis_index("y")]).astype(jnp.int32)
    turned = turn(head_outputs)
    heads = lax.all_gather(turned, "y", axis=0, tiled=True)
    masked = cotangent * loss_mask[:, None].astype(bf16)
    pieces = masked.reshape(128, 8, 2, 288).transpose(1, 2, 3, 0)
    low, high = pieces[:, 0], pieces[:, 1]
    ordered = jnp.concatenate(
        [jnp.where(xl == 0, low, high), jnp.where(xl == 0, high, low)], axis=1
    )
    arrived = turn(lax.all_to_all(ordered, "y", split_axis=0, concat_axis=0, tiled=True))
    weight_t, own_gain, _ = lax.optimization_barrier((out_weight.T, norm_gain, turned))
    weight_got, gain_got = swap(weight_t, "xl"), swap(own_gain, "xl")
    straight = xl == core
    weights = jnp.concatenate(
        [jnp.where(straight, weight_t, weight_got), jnp.where(straight, weight_got, weight_t)], axis=0
    )
    gain = jnp.concatenate(
        [jnp.where(straight, own_gain, gain_got), jnp.where(straight, gain_got, own_gain)]
    )
    heads, weights, arrived, gain = lax.optimization_barrier((heads, weights, arrived, gain))
    gain = gain[:, None]
    other_heads = swap(heads, "core")
    cotangents = arrived.transpose(1, 0, 2).reshape(576, 1024).astype(f32)
    projected = lax.dot_general(
        weights, heads, (((1,), (1,)), ((), ())), preferred_element_type=f32
    )
    stats = jnp.stack(
        [jnp.sum(projected * projected, axis=0), jnp.sum(projected * gain * cotangents, axis=0)]
    )
    stats = lax.all_to_all(
        jnp.broadcast_to(stats[None], (8, 2, 1024)), "y", split_axis=0, concat_axis=0, tiled=True
    )
    got_grad = swap(gradients(True, projected, arrived, gain, stats)[0], "core")
    keep_grad, gain_keep = gradients(False, projected, arrived, gain, stats)
    *packed, squares = deltas(place, keep_grad, got_grad, gain_keep, heads, other_heads)
    parts = [to_owner(x, *slot) for x, slot in zip(packed, SLOTS)]
    sums = lax.all_to_all(squares, ("xh", "core", "y", "xl"), split_axis=0, concat_axis=0, tiled=True)
    chip = combine(place, sums, parts)
    over_z = lax.all_to_all(chip, "z", split_axis=0, concat_axis=0, tiled=True)
    update, gain_update = finish(over_z, weight_noise, lanes(gain_noise))
    return update, gain_update.reshape(384)[:288]


def solution(mesh):
    split_mesh = Mesh(mesh.devices.reshape(2, 8, 2, 8, 2), CLIENT + FSDP)
    both = CLIENT + FSDP
    placed = (
        P(both, None),
        P(None, FSDP),
        P(FSDP),
        P(both, None),
        P(both),
        P(CLIENT, FSDP),
        P(FSDP),
    )
    return jax.shard_map(
        local,
        mesh=split_mesh,
        in_specs=placed,
        out_specs=(P(CLIENT, FSDP), P(FSDP)),
        check_vma=False,
    )
```

```python
import functools
import functools
import math

import jax
import jax.numpy as jnp
from jax import lax
from jax.experimental import pallas as pl
from jax.experimental.pallas import tpu as pltpu
from jax.sharding import Mesh, PartitionSpec as P

D = 4608
HD = 2048
epsilon = 1e-06
CLIENT = ("xh", "z", "core")
FSDP = ("y", "xl")
BOUND = math.sqrt(HD * D)
f32 = jnp.float32
bf16 = jnp.bfloat16


def swap(x, axis):
    return lax.ppermute(x, axis, [(0, 1), (1, 0)])


def full(shape):
    return pl.BlockSpec(shape, lambda *i: (0,) * len(shape))


def place_spec():
    return pl.BlockSpec(memory_space=pltpu.SMEM)


def whole():
    return pl.BlockSpec(memory_space=pltpu.VMEM)


SLOTS = ((1, 0), (1, 1), (0, 0), (0, 1))


def grad_kernel(sent, proj_ref, masked_ref, gain_ref, stats_ref, out_ref, *rest):
    total = rest[-1]
    step = pl.program_id(0)
    stats = stats_ref[0]
    for i in range(1, 8):
        stats = stats + stats_ref[i]
    inverse = lax.rsqrt(stats[0:1] / D + epsilon)
    coefficient = inverse * inverse * inverse * stats[1:2] / D

    def part(first):
        for start in range(0, 144, 48):
            rows = slice(start, start + 48)
            gain = jnp.broadcast_to(gain_ref[rows], (48, 128))
            summed = jnp.zeros((48, 128), f32)
            for i in range(8):
                lane = slice(128 * i, 128 * i + 128)
                p = proj_ref[rows, lane]
                m = masked_ref[i, rows].astype(f32) * inverse[:, lane]
                out_ref[first + start : first + start + 48, lane] = (gain * m - p * coefficient[:, lane]).astype(bf16)
                summed += m * p
            total[first + start : first + start + 48] = summed

    for n in range(2):

        @pl.when(step == n)
        def _(n=n):
            part(144 * n)

    @pl.when(step == 1)
    def _():
        row = jnp.sum(total[...].T, axis=0, keepdims=True)
        row = jnp.concatenate([row, jnp.zeros((1, 96), f32)], axis=1)
        gain = jnp.concatenate([row[:, 0:128], row[:, 128:256], row[:, 256:384]], axis=0)
        if sent:
            high = gain.astype(bf16).astype(f32)
            extra = jnp.concatenate([high, gain - high, jnp.zeros((10, 128), f32)], axis=0).astype(bf16)
            for i in range(8):
                out_ref[288:, 128 * i : 128 * i + 128] = extra
        else:
            rest[0][...] = gain


def gradients(sent, projected, masked, gain, stats):
    base = 2 if sent else 0
    rows = 304 if sent else 288
    outs = [((rows, 1024), bf16)] + ([] if sent else [((3, 128), f32)])
    return pl.pallas_call(
        functools.partial(grad_kernel, sent),
        grid=(2,),
        in_specs=[
            pl.BlockSpec((144, 1024), lambda n: (base + n, 0)),
            pl.BlockSpec((8, 144, 128), lambda n: (0, base + n, 0)),
            pl.BlockSpec((144, 1), lambda n: (base + n, 0)),
            full((8, 2, 1024)),
        ],
        out_specs=[full(shape) for shape, _ in outs],
        out_shape=[jax.ShapeDtypeStruct(shape, kind) for shape, kind in outs],
        scratch_shapes=[pltpu.VMEM((288, 128), f32)],
        cost_estimate=pl.CostEstimate(flops=4000000, bytes_accessed=6000000, transcendentals=0),
        name="gradients_sent" if sent else "gradients_kept",
    )(projected, masked, gain, stats)


def delta_kernel(far, place_ref, keep_ref, got_ref, *rest):
    if far:
        heads_ref, other_ref, same_ref, flip_ref, sum_ref, total = rest
    else:
        gain_ref, far_ref, heads_ref, other_ref, same_ref, flip_ref, sum_ref, total = rest
    step = pl.program_id(0)
    value = jnp.dot(keep_ref[...], heads_ref[...], preferred_element_type=f32)
    value = value + jnp.dot(got_ref[:288], other_ref[...], preferred_element_type=f32)
    folded = jnp.zeros((288, 128), f32)
    for j in range(4):
        folded += value[:, 128 * j : 128 * j + 128] * value[:, 128 * j : 128 * j + 128]
    left = lax.broadcasted_iota(jnp.int32, (288, 128), 1) < 64
    zero = place_ref[1] == 0

    def pack(n):
        for j in range(2):
            a, b = value[:, 256 * j : 256 * j + 128], value[:, 256 * j + 128 : 256 * j + 256]
            first = jnp.where(left, a, pltpu.roll(b, 64, 1))
            second = jnp.where(left, pltpu.roll(a, 64, 1), b)
            lane = slice(256 * n + j * 128, 256 * n + j * 128 + 128)
            same_ref[:, lane] = jnp.where(zero, first, second).astype(bf16)
            flip_ref[:, lane] = jnp.where(zero, second, first).astype(bf16)

    @pl.when(step == 0)
    def _():
        total[...] = folded
        pack(0)

    @pl.when(step == 1)
    def _():
        total[...] += folded
        pack(1)
        if far:
            sum_ref[...] = jnp.sum(total[...], axis=0, keepdims=True)
        else:
            extra = got_ref[288:, :128].astype(f32)
            gain = gain_ref[...] + extra[0:3] + extra[3:6]
            norm = jnp.sum(total[...]) + jnp.sum(far_ref[...]) + jnp.sum(gain * gain)
            tile = jnp.concatenate([jnp.full((1, 128), norm, f32), gain, jnp.zeros((4, 128), f32)], axis=0)
            for i in range(64):
                sum_ref[i] = tile


def deltas(far, place, keep, got, heads, *more):
    fixed = lambda shape: pl.BlockSpec(shape, lambda n, place: (0,) * len(shape))
    columns = pl.BlockSpec((1024, 512), lambda n, place: (0, (place[0] ^ far) * 2 + n))
    packed = jax.ShapeDtypeStruct((288, 512), bf16)
    sums = (1, 128) if far else (64, 8, 128)
    return pl.pallas_call(
        functools.partial(delta_kernel, far),
        grid_spec=pltpu.PrefetchScalarGridSpec(
            num_scalar_prefetch=1,
            grid=(2,),
            in_specs=[whole()] * (2 + len(more)) + [columns, columns],
            out_specs=[fixed((288, 512))] * 2 + [fixed(sums)],
            scratch_shapes=[pltpu.VMEM((288, 128), f32)],
        ),
        out_shape=[packed] * 2 + [jax.ShapeDtypeStruct(sums, f32)],
        cost_estimate=pl.CostEstimate(flops=2 * 288 * 1024 * 2048, bytes_accessed=6000000, transcendentals=0),
        name="deltas_far" if far else "deltas_near",
    )(place, keep, got, *more, *heads)


def combine_kernel(place_ref, sums_ref, a_ref, b_ref, c_ref, d_ref, out_ref):
    odd = lax.broadcasted_iota(jnp.int32, (32, 128), 0) % 2
    factors = []
    for h in range(2):
        rows = sums_ref[32 * h : 32 * h + 32, 0]
        for p in range(2):
            norm = jnp.sum(jnp.where(odd == p, rows, 0.0), axis=0, keepdims=True)
            factors.append(BOUND / jnp.maximum(jnp.sqrt(norm), BOUND))
    high_zero = place_ref[0] == 0
    core_zero = place_ref[2] == 0
    weights = []
    for d, c in SLOTS:
        pair = [jnp.where(high_zero, factors[2 * d + p], factors[2 - 2 * d + p]) for p in range(2)]
        weights.append(jnp.where(core_zero, pair[c], pair[1 - c]))
    refs = (a_ref, b_ref, c_ref, d_ref)

    def weighted(rows, lane):
        total = weights[0] * refs[0][rows, lane].astype(f32)
        for w, ref in zip(weights[1:], refs[1:]):
            total = total + w * ref[rows, lane].astype(f32)
        return total

    gain = jnp.zeros((3, 128), f32)
    for w, (d, c) in zip(weights, SLOTS):
        row = (place_ref[0] ^ d) * 32 + place_ref[1] * 16 + place_ref[3] * 2 + (place_ref[2] ^ c)
        gain = gain + w * sums_ref[row][1:4]
    high = gain.astype(bf16).astype(f32)
    extra = jnp.concatenate([high, gain - high, jnp.zeros((10, 128), f32)], axis=0).astype(bf16)
    left = lax.broadcasted_iota(jnp.int32, (144, 128), 1) < 64
    for j in range(4):
        part = weighted(slice(0, 288), slice(j * 128, j * 128 + 128))
        low, up = part[:144], part[144:]
        out_ref[2 * j, :144] = jnp.where(left, low, pltpu.roll(up, 64, 1)).astype(bf16)
        out_ref[2 * j + 1, :144] = jnp.where(left, pltpu.roll(low, 64, 1), up).astype(bf16)
        out_ref[2 * j, 144:] = extra
        out_ref[2 * j + 1, 144:] = extra


def combine(place, sums, parts):
    return pl.pallas_call(
        combine_kernel,
        in_specs=[place_spec()] + [whole()] * 5,
        out_specs=whole(),
        out_shape=jax.ShapeDtypeStruct((8, 160, 128), bf16),
        name="clip_and_combine",
    )(place, sums, *parts)


def finish_kernel(parts_ref, noise_ref, gain_noise_ref, out_ref, gain_ref):
    total = parts_ref[0].astype(f32)
    for i in range(1, 8):
        total = total + parts_ref[i].astype(f32)
    body = total[:144]
    rows = jnp.concatenate([body, pltpu.roll(body, 64, 1)], axis=0).T
    out_ref[...] = (rows[:64] + noise_ref[...]) * (1.0 / 32.0)
    gain_ref[...] = (total[144:147] + total[147:150] + gain_noise_ref[...]) * (1.0 / 32.0)


def finish(parts, noise, gain_noise):
    return pl.pallas_call(
        finish_kernel,
        out_shape=[jax.ShapeDtypeStruct((64, 288), f32), jax.ShapeDtypeStruct((3, 128), f32)],
        name="sum_and_noise",
    )(parts, noise, gain_noise)


def lanes(vector):
    return jnp.pad(vector, (0, 96)).reshape(3, 128)


def turn(x):
    return lax.ppermute(x, ("core", "xl"), [(0, 0), (1, 2), (2, 1), (3, 3)])


def to_owner(x, flip_high, flip_core):
    pairs = []
    for h in range(2):
        for c in range(2):
            for p in range(2):
                pairs.append((h * 4 + c * 2 + p, (h ^ flip_high) * 4 + (p ^ flip_core) * 2 + c))
    return lax.ppermute(x, ("xh", "core", "xl"), pairs)


def local(head_outputs, out_weight, norm_gain, cotangent, loss_mask, weight_noise, gain_noise):
    xl = lax.axis_index("xl")
    core = lax.axis_index("core")
    place = jnp.stack([lax.axis_index("xh"), xl, core, lax.axis_index("y")]).astype(jnp.int32)
    turned = turn(head_outputs)
    heads = lax.all_gather(turned, "y", axis=0, tiled=True)
    masked = cotangent * loss_mask[:, None].astype(bf16)
    pieces = masked.reshape(128, 8, 2, 288).transpose(1, 2, 3, 0)
    low, high = pieces[:, 0], pieces[:, 1]
    ordered = jnp.concatenate(
        [jnp.where(xl == 0, low, high), jnp.where(xl == 0, high, low)], axis=1
    )
    arrived = turn(lax.all_to_all(ordered, "y", split_axis=0, concat_axis=0, tiled=True))
    weight_t, own_gain, _ = lax.optimization_barrier((out_weight.T, norm_gain, turned))
    weight_got, gain_got = swap(weight_t, "xl"), swap(own_gain, "xl")
    straight = xl == core
    weights = jnp.concatenate(
        [jnp.where(straight, weight_t, weight_got), jnp.where(straight, weight_got, weight_t)], axis=0
    )
    gain = jnp.concatenate(
        [jnp.where(straight, own_gain, gain_got), jnp.where(straight, gain_got, own_gain)]
    )
    heads, weights, arrived, gain = lax.optimization_barrier((heads, weights, arrived, gain))
    gain = gain[:, None]
    other_heads = swap(heads, "core")
    cotangents = arrived.transpose(1, 0, 2).reshape(576, 1024).astype(f32)
    projected = lax.dot_general(
        weights, heads, (((1,), (1,)), ((), ())), preferred_element_type=f32
    )
    stats = jnp.stack(
        [jnp.sum(projected * projected, axis=0), jnp.sum(projected * gain * cotangents, axis=0)]
    )
    stats = lax.all_to_all(
        jnp.broadcast_to(stats[None], (8, 2, 1024)), "y", split_axis=0, concat_axis=0, tiled=True
    )
    got_grad = swap(gradients(True, projected, arrived, gain, stats)[0], "core")
    keep_grad, gain_keep = gradients(False, projected, arrived, gain, stats)
    both = (heads, other_heads)
    a, b, far_sum = deltas(1, place, keep_grad, got_grad, both)
    c, d, squares = deltas(0, place, keep_grad, got_grad, both, gain_keep, far_sum)
    a, b, c, d = lax.optimization_barrier((to_owner(a, *SLOTS[0]), to_owner(b, *SLOTS[1]), c, d))
    parts = [a, b, to_owner(c, *SLOTS[2]), to_owner(d, *SLOTS[3])]
    sums = lax.all_to_all(squares, ("xh", "core", "y", "xl"), split_axis=0, concat_axis=0, tiled=True)
    chip = combine(place, sums, parts)
    over_z = lax.all_to_all(chip, "z", split_axis=0, concat_axis=0, tiled=True)
    update, gain_update = finish(over_z, weight_noise, lanes(gain_noise))
    return update, gain_update.reshape(384)[:288]


def solution(mesh):
    split_mesh = Mesh(mesh.devices.reshape(2, 8, 2, 8, 2), CLIENT + FSDP)
    both = CLIENT + FSDP
    placed = (
        P(both, None),
        P(None, FSDP),
        P(FSDP),
        P(both, None),
        P(both),
        P(CLIENT, FSDP),
        P(FSDP),
    )
    return jax.shard_map(
        local,
        mesh=split_mesh,
        in_specs=placed,
        out_specs=(P(CLIENT, FSDP), P(FSDP)),
        check_vma=False,
    )
```

```python
import functools
import functools
import math

import jax
import jax.numpy as jnp
from jax import lax
from jax.experimental import pallas as pl
from jax.experimental.pallas import tpu as pltpu
from jax.sharding import Mesh, PartitionSpec as P

D = 4608
HD = 2048
epsilon = 1e-06
CLIENT = ("xh", "z", "core")
FSDP = ("y", "xl")
BOUND = math.sqrt(HD * D)
f32 = jnp.float32
bf16 = jnp.bfloat16


def swap(x, axis):
    return lax.ppermute(x, axis, [(0, 1), (1, 0)])


def full(shape):
    return pl.BlockSpec(shape, lambda *i: (0,) * len(shape))


def place_spec():
    return pl.BlockSpec(memory_space=pltpu.SMEM)


def whole():
    return pl.BlockSpec(memory_space=pltpu.VMEM)


SLOTS = ((1, 0), (1, 1), (0, 0), (0, 1))


def grad_kernel(sent, proj_ref, masked_ref, gain_ref, stats_ref, out_ref, *rest):
    total = rest[-1]
    step = pl.program_id(0)
    stats = stats_ref[0]
    for i in range(1, 8):
        stats = stats + stats_ref[i]
    inverse = lax.rsqrt(stats[0:1] / D + epsilon)
    coefficient = inverse * inverse * inverse * stats[1:2] / D

    def part(first):
        for start in range(0, 144, 48):
            rows = slice(start, start + 48)
            gain = jnp.broadcast_to(gain_ref[rows], (48, 128))
            summed = jnp.zeros((48, 128), f32)
            for i in range(8):
                lane = slice(128 * i, 128 * i + 128)
                p = proj_ref[rows, lane]
                m = masked_ref[i, rows].astype(f32) * inverse[:, lane]
                out_ref[first + start : first + start + 48, lane] = (gain * m - p * coefficient[:, lane]).astype(bf16)
                summed += m * p
            total[first + start : first + start + 48] = summed

    for n in range(2):

        @pl.when(step == n)
        def _(n=n):
            part(144 * n)

    @pl.when(step == 1)
    def _():
        row = jnp.sum(total[...].T, axis=0, keepdims=True)
        row = jnp.concatenate([row, jnp.zeros((1, 96), f32)], axis=1)
        gain = jnp.concatenate([row[:, 0:128], row[:, 128:256], row[:, 256:384]], axis=0)
        if sent:
            high = gain.astype(bf16).astype(f32)
            extra = jnp.concatenate([high, gain - high, jnp.zeros((10, 128), f32)], axis=0).astype(bf16)
            for i in range(8):
                out_ref[288:, 128 * i : 128 * i + 128] = extra
        else:
            rest[0][...] = gain


def gradients(sent, projected, masked, gain, stats):
    base = 2 if sent else 0
    rows = 304 if sent else 288
    outs = [((rows, 1024), bf16)] + ([] if sent else [((3, 128), f32)])
    return pl.pallas_call(
        functools.partial(grad_kernel, sent),
        grid=(2,),
        in_specs=[
            pl.BlockSpec((144, 1024), lambda n: (base + n, 0)),
            pl.BlockSpec((8, 144, 128), lambda n: (0, base + n, 0)),
            pl.BlockSpec((144, 1), lambda n: (base + n, 0)),
            full((8, 2, 1024)),
        ],
        out_specs=[full(shape) for shape, _ in outs],
        out_shape=[jax.ShapeDtypeStruct(shape, kind) for shape, kind in outs],
        scratch_shapes=[pltpu.VMEM((288, 128), f32)],
        cost_estimate=pl.CostEstimate(flops=4000000, bytes_accessed=6000000, transcendentals=0),
        name="gradients_sent" if sent else "gradients_kept",
    )(projected, masked, gain, stats)


def delta_kernel(place_ref, keep_ref, got_ref, gain_ref, heads_ref, other_ref, *rest):
    outs, sum_ref, total = rest[:4], rest[4], rest[5]
    step = pl.program_id(0)
    value = jnp.dot(keep_ref[...], heads_ref[...], preferred_element_type=f32)
    value = value + jnp.dot(got_ref[:288], other_ref[...], preferred_element_type=f32)
    folded = jnp.zeros((288, 128), f32)
    for j in range(8):
        folded += value[:, 128 * j : 128 * j + 128] * value[:, 128 * j : 128 * j + 128]
    left = lax.broadcasted_iota(jnp.int32, (288, 128), 1) < 64
    zero = place_ref[1] == 0

    def pack(d):
        for j in range(4):
            a, b = value[:, 256 * j : 256 * j + 128], value[:, 256 * j + 128 : 256 * j + 256]
            first = jnp.where(left, a, pltpu.roll(b, 64, 1))
            second = jnp.where(left, pltpu.roll(a, 64, 1), b)
            lane = slice(j * 128, j * 128 + 128)
            outs[SLOTS.index((d, 0))][:, lane] = jnp.where(zero, first, second).astype(bf16)
            outs[SLOTS.index((d, 1))][:, lane] = jnp.where(zero, second, first).astype(bf16)

    @pl.when(step == 0)
    def _():
        total[...] = folded
        pack(1)

    @pl.when(step == 1)
    def _():
        total[...] += folded
        pack(0)

    @pl.when(step == 1)
    def _():
        extra = got_ref[288:, :128].astype(f32)
        gain = gain_ref[...] + extra[0:3] + extra[3:6]
        norm = jnp.sum(total[...]) + jnp.sum(gain * gain)
        tile = jnp.concatenate([jnp.full((1, 128), norm, f32), gain, jnp.zeros((4, 128), f32)], axis=0)
        for i in range(64):
            sum_ref[i] = tile


def deltas(place, keep, got, gain, heads, other_heads):
    fixed = lambda shape: pl.BlockSpec(shape, lambda n, place: (0,) * len(shape))
    columns = pl.BlockSpec((1024, 1024), lambda n, place: (0, place[0] ^ (1 - n)))
    packed = jax.ShapeDtypeStruct((288, 512), bf16)
    return pl.pallas_call(
        delta_kernel,
        grid_spec=pltpu.PrefetchScalarGridSpec(
            num_scalar_prefetch=1,
            grid=(2,),
            in_specs=[fixed((288, 1024)), fixed((304, 1024)), fixed((3, 128)), columns, columns],
            out_specs=[fixed((288, 512))] * 4 + [fixed((64, 8, 128))],
            scratch_shapes=[pltpu.VMEM((288, 128), f32)],
        ),
        out_shape=[packed] * 4 + [jax.ShapeDtypeStruct((64, 8, 128), f32)],
        cost_estimate=pl.CostEstimate(flops=4 * 288 * 1024 * 2048, bytes_accessed=12000000, transcendentals=0),
        name="deltas",
    )(place, keep, got, gain, heads, other_heads)


def combine_kernel(place_ref, sums_ref, a_ref, b_ref, c_ref, d_ref, out_ref):
    odd = lax.broadcasted_iota(jnp.int32, (32, 128), 0) % 2
    factors = []
    for h in range(2):
        rows = sums_ref[32 * h : 32 * h + 32, 0]
        for p in range(2):
            norm = jnp.sum(jnp.where(odd == p, rows, 0.0), axis=0, keepdims=True)
            factors.append(BOUND / jnp.maximum(jnp.sqrt(norm), BOUND))
    high_zero = place_ref[0] == 0
    core_zero = place_ref[2] == 0
    weights = []
    for d, c in SLOTS:
        pair = [jnp.where(high_zero, factors[2 * d + p], factors[2 - 2 * d + p]) for p in range(2)]
        weights.append(jnp.where(core_zero, pair[c], pair[1 - c]))
    refs = (a_ref, b_ref, c_ref, d_ref)

    def weighted(rows, lane):
        total = weights[0] * refs[0][rows, lane].astype(f32)
        for w, ref in zip(weights[1:], refs[1:]):
            total = total + w * ref[rows, lane].astype(f32)
        return total

    gain = jnp.zeros((3, 128), f32)
    for w, (d, c) in zip(weights, SLOTS):
        row = (place_ref[0] ^ d) * 32 + place_ref[1] * 16 + place_ref[3] * 2 + (place_ref[2] ^ c)
        gain = gain + w * sums_ref[row][1:4]
    high = gain.astype(bf16).astype(f32)
    extra = jnp.concatenate([high, gain - high, jnp.zeros((10, 128), f32)], axis=0).astype(bf16)
    left = lax.broadcasted_iota(jnp.int32, (144, 128), 1) < 64
    for j in range(4):
        part = weighted(slice(0, 288), slice(j * 128, j * 128 + 128))
        low, up = part[:144], part[144:]
        out_ref[2 * j, :144] = jnp.where(left, low, pltpu.roll(up, 64, 1)).astype(bf16)
        out_ref[2 * j + 1, :144] = jnp.where(left, pltpu.roll(low, 64, 1), up).astype(bf16)
        out_ref[2 * j, 144:] = extra
        out_ref[2 * j + 1, 144:] = extra


def combine(place, sums, parts):
    return pl.pallas_call(
        combine_kernel,
        in_specs=[place_spec()] + [whole()] * 5,
        out_specs=whole(),
        out_shape=jax.ShapeDtypeStruct((8, 160, 128), bf16),
        name="clip_and_combine",
    )(place, sums, *parts)


def finish_kernel(parts_ref, noise_ref, gain_noise_ref, out_ref, gain_ref):
    total = parts_ref[0].astype(f32)
    for i in range(1, 8):
        total = total + parts_ref[i].astype(f32)
    body = total[:144]
    rows = jnp.concatenate([body, pltpu.roll(body, 64, 1)], axis=0).T
    out_ref[...] = (rows[:64] + noise_ref[...]) * (1.0 / 32.0)
    gain_ref[...] = (total[144:147] + total[147:150] + gain_noise_ref[...]) * (1.0 / 32.0)


def finish(parts, noise, gain_noise):
    return pl.pallas_call(
        finish_kernel,
        out_shape=[jax.ShapeDtypeStruct((64, 288), f32), jax.ShapeDtypeStruct((3, 128), f32)],
        name="sum_and_noise",
    )(parts, noise, gain_noise)


def lanes(vector):
    return jnp.pad(vector, (0, 96)).reshape(3, 128)


def turn(x):
    return lax.ppermute(x, ("core", "xl"), [(0, 0), (1, 2), (2, 1), (3, 3)])


def to_owner(x, flip_high, flip_core):
    pairs = []
    for h in range(2):
        for c in range(2):
            for p in range(2):
                pairs.append((h * 4 + c * 2 + p, (h ^ flip_high) * 4 + (p ^ flip_core) * 2 + c))
    return lax.ppermute(x, ("xh", "core", "xl"), pairs)


def local(head_outputs, out_weight, norm_gain, cotangent, loss_mask, weight_noise, gain_noise):
    xl = lax.axis_index("xl")
    core = lax.axis_index("core")
    place = jnp.stack([lax.axis_index("xh"), xl, core, lax.axis_index("y")]).astype(jnp.int32)
    turned = turn(head_outputs)
    heads = lax.all_gather(turned, "y", axis=0, tiled=True)
    masked = cotangent * loss_mask[:, None].astype(bf16)
    pieces = masked.reshape(128, 8, 2, 288).transpose(1, 2, 3, 0)
    low, high = pieces[:, 0], pieces[:, 1]
    ordered = jnp.concatenate(
        [jnp.where(xl == 0, low, high), jnp.where(xl == 0, high, low)], axis=1
    )
    arrived = turn(lax.all_to_all(ordered, "y", split_axis=0, concat_axis=0, tiled=True))
    weight_t, own_gain, _ = lax.optimization_barrier((out_weight.T, norm_gain, turned))
    weight_got, gain_got = swap(weight_t, "xl"), swap(own_gain, "xl")
    straight = xl == core
    weights = jnp.concatenate(
        [jnp.where(straight, weight_t, weight_got), jnp.where(straight, weight_got, weight_t)], axis=0
    )
    gain = jnp.concatenate(
        [jnp.where(straight, own_gain, gain_got), jnp.where(straight, gain_got, own_gain)]
    )
    heads, weights, arrived, gain = lax.optimization_barrier((heads, weights, arrived, gain))
    gain = gain[:, None]
    other_heads = swap(heads, "core")
    cotangents = arrived.transpose(1, 0, 2).reshape(576, 1024).astype(f32)
    projected = lax.dot_general(
        weights, heads, (((1,), (1,)), ((), ())), preferred_element_type=f32
    )
    stats = jnp.stack(
        [jnp.sum(projected * projected, axis=0), jnp.sum(projected * gain * cotangents, axis=0)]
    )
    stats = lax.all_to_all(
        jnp.broadcast_to(stats[None], (8, 2, 1024)), "y", split_axis=0, concat_axis=0, tiled=True
    )
    got_grad = swap(gradients(True, projected, arrived, gain, stats)[0], "core")
    keep_grad, gain_keep = gradients(False, projected, arrived, gain, stats)
    *packed, squares = deltas(place, keep_grad, got_grad, gain_keep, heads, other_heads)
    parts = [to_owner(x, *slot) for x, slot in zip(packed, SLOTS)]
    sums = lax.all_to_all(squares, ("xh", "core", "y", "xl"), split_axis=0, concat_axis=0, tiled=True)
    chip = combine(place, sums, parts)
    over_z = lax.all_to_all(chip, "z", split_axis=0, concat_axis=0, tiled=True)
    update, gain_update = finish(over_z, weight_noise, lanes(gain_noise))
    return update, gain_update.reshape(384)[:288]


def solution(mesh):
    split_mesh = Mesh(mesh.devices.reshape(2, 8, 2, 8, 2), CLIENT + FSDP)
    both = CLIENT + FSDP
    placed = (
        P(both, None),
        P(None, FSDP),
        P(FSDP),
        P(both, None),
        P(both),
        P(CLIENT, FSDP),
        P(FSDP),
    )
    return jax.shard_map(
        local,
        mesh=split_mesh,
        in_specs=placed,
        out_specs=(P(CLIENT, FSDP), P(FSDP)),
        check_vma=False,
    )
```
